32 devices in a mesh: rep: 2 (over y), tm: 4 (over z), tk: 4 (over x, core).
Axes of the slice: x: 2, y: 2, z: 4, core: 2. Of those that a mesh axis runs over, the one named last changes fastest.
Arguments:
- hidden_in: bfloat16 [2, 128, 8192], P(None, ('rep', 'tm'), 'tk'), parts along dimension 1, may hold values from -6 to 6
- gate_weight: bfloat16 [8192, 28672], P('tk', 'tm'), may hold values from -0.0625 to 0.0625
- up_weight: bfloat16 [8192, 28672], P('tk', 'tm'), may hold values from -0.0625 to 0.0625
- shrink_store: bfloat16 [4, 8192, 128], P('tm', 'tk'), may hold values from -0.0625 to 0.0625
- expand_gate: bfloat16 [4, 64, 28672], P('tk', None, 'tm'), may hold values from -0.75 to 0.75
- expand_up: bfloat16 [4, 64, 28672], P('tk', None, 'tm'), may hold values from -0.75 to 0.75
- block_adapter: int32 [2, 16], P(None, 'rep'), parts along dimension 1, may hold values from 0 to 3
- store_slot: int32 [4], replicated, may hold values from 0 to 3, each once
Outputs:
- activated: bfloat16 [128, 2, 28672], P(('rep', 'tk'), None, 'tm'), parts along dimension 0
The draws below stay inside these ranges and needn't reach their ends.
There are 2 independent parts, one for each index of `rep`. The reference program is written for one: setup_inputs(seed, part) draws one part's arguments, and reference() takes and returns one part's arrays. A program takes and returns all parts, laid end to end along the dimension named above; an argument that names none is the same for every part. Nothing has to cross between parts.
Inputs may be any that keep to these rules, and one draw needn't show every extreme that they name: store_slot names every store position once; position p lies with index p // 1 of tm.
All inputs are finite; a program needn't handle non-finite values.
Results may differ from the reference program's by a relative error of at most 0.0049.
Values may be sent and summed in bfloat16 or wider, within the bound.
No kernel may reach another device: no remote copies, remote signals or barrier semaphores. Data moves between devices by JAX's collectives and lax.ppermute only.
A program may use at most 192 MiB of HBM per device.

```python
import math
import jax
import jax.numpy as jnp
import numpy as np
from jax import lax

D = 8192
FF = 28672
RANK = 64
BLOCK = 8
STEPS = 2
ADAPTERS = 4
ROWS = 64
BLOCKS = 8


def place_ends(entries, rng, low, largest):
    extent = entries.shape
    place = [jax.random.randint(jax.random.fold_in(rng, axis), (), 0, extent[axis]) for axis in range(len(extent))]
    entries = entries.at[tuple(place)].set(low)
    longest = extent.index(max(extent))
    place[longest] = (place[longest] + 1) % extent[longest]
    return entries.at[tuple(place)].set(largest)


def block_scale(rng, shape, cuts, least, top_value):
    def one(dim, blocks):
        steps = jax.random.uniform(jax.random.fold_in(jax.random.fold_in(rng, 6), dim), (blocks,), jnp.float32, least / len(cuts), top_value / len(cuts))
        return jnp.repeat(jnp.exp(steps), shape[dim] // blocks).reshape((-1,) + (1,) * (len(shape) - dim - 1))

    factor_of = one(*cuts[0])
    for cut in cuts[1:]:
        factor_of = factor_of * one(*cut)
    return factor_of


def rank_bounds(number_of, slope):
    portions = [(1 << 20) // math.isqrt(rank ** slope) + 1 for rank in range(1, number_of + 1)]
    scale = 1 + sum(portions) // (1 << 30)
    return np.cumsum(np.array([max(1, weight // scale) for weight in portions]))


def skewed_ids(own_key, dims, number_of, lean):
    table = rank_bounds(number_of, lean)
    pick = jax.random.randint(jax.random.fold_in(own_key, 1), dims, 0, int(table[number_of - 1]))
    rank = jnp.searchsorted(jnp.asarray(table, jnp.int32), pick, side="right")
    return jax.random.permutation(jax.random.fold_in(own_key, 2), number_of)[rank].astype(jnp.int32)


def scatter_about(key, extent, scale, reach, pieces=(), dtype=jnp.bfloat16):
    values = scale * jax.random.normal(key, extent, jnp.float32)
    if pieces:
        values = values * block_scale(key, extent, pieces, -0.22, 0.18)
    return jnp.clip(values, -reach, reach).astype(dtype)


def setup_inputs(seed: int = 0, part: int = 0) -> dict:
    seeds = jax.random.split(jax.random.key(seed), 9)
    own_keys = jax.random.split(jax.random.fold_in(seeds[8], part), 9)
    return {
        "hidden_in": scatter_about(own_keys[0], (STEPS, ROWS, D), 1.0, 6.0, ((1, 4), (2, 4))),
        "gate_weight": scatter_about(seeds[1], (D, FF), D ** -0.5, 0.0625, ((0, 4), (1, 4))),
        "up_weight": scatter_about(seeds[2], (D, FF), D ** -0.5, 0.0625, ((0, 4), (1, 4))),
        "shrink_store": scatter_about(seeds[3], (ADAPTERS, D, 2 * RANK), D ** -0.5, 0.0625, ((0, 4), (1, 4))),
        "expand_gate": scatter_about(seeds[4], (ADAPTERS, RANK, FF), RANK ** -0.5, 0.75, ((0, 4), (2, 4))),
        "expand_up": scatter_about(seeds[5], (ADAPTERS, RANK, FF), RANK ** -0.5, 0.75, ((0, 4), (2, 4))),
        "block_adapter": place_ends(skewed_ids(own_keys[6], (STEPS, BLOCKS), ADAPTERS, 2), jax.random.fold_in(own_keys[6], 3), 0, ADAPTERS - 1).astype(jnp.int32),
        "store_slot": jax.random.permutation(seeds[7], ADAPTERS).astype(jnp.int32),
    }


def reference(hidden_in, gate_weight, up_weight, shrink_store, expand_gate, expand_up, block_adapter, store_slot):
    block_slot = jnp.take(store_slot, block_adapter.reshape(-1)).astype(jnp.int32)
    blocks = hidden_in.reshape(STEPS * BLOCKS, BLOCK, D)

    def adapt(item):
        rows, slot = item
        shrunk = jnp.dot(rows, shrink_store[slot], preferred_element_type=jnp.float32).astype(jnp.bfloat16)
        gate_delta = jnp.dot(shrunk[:, :RANK], expand_gate[slot], preferred_element_type=jnp.float32)
        up_delta = jnp.dot(shrunk[:, RANK:], expand_up[slot], preferred_element_type=jnp.float32)
        return gate_delta, up_delta

    gate_delta, up_delta = lax.map(adapt, (blocks, block_slot))
    flat = hidden_in.reshape(STEPS * ROWS, D)
    gate_pre = jnp.dot(flat, gate_weight, preferred_element_type=jnp.float32) + gate_delta.reshape(STEPS * ROWS, FF)
    up_pre = jnp.dot(flat, up_weight, preferred_element_type=jnp.float32) + up_delta.reshape(STEPS * ROWS, FF)
    activated = (jax.nn.silu(gate_pre) * up_pre).astype(jnp.bfloat16).reshape(STEPS, ROWS, FF)
    return jnp.transpose(activated, (1, 0, 2))
```

```python
import functools

import jax
import jax.numpy as jnp
from jax import lax
from jax.experimental import pallas as pl
from jax.experimental.pallas import tpu as pltpu
from jax.sharding import PartitionSpec as P

BLOCK = 8
MIB = 2**20
F32 = jnp.float32
BF16 = jnp.bfloat16
CHUNKS = (1024, 2048, 2048, 2048)
TILE = 256


def slots_of_rows(block_adapter, store_slot):
    count = store_slot.shape[0]
    match = block_adapter[:, :, None] == jnp.arange(count, dtype=jnp.int32)
    block_slot = jnp.sum(jnp.where(match, store_slot, 0), axis=2)
    return jnp.repeat(block_slot, BLOCK, axis=1)


def shrink_part(gathered, row_slot, shrink_store):
    owned = shrink_store.shape[0]
    first = lax.axis_index("tm") * owned
    product = jnp.einsum(
        "srd,adk->srak", gathered, shrink_store, preferred_element_type=F32
    )
    chosen = row_slot[:, :, None] == first + jnp.arange(owned, dtype=jnp.int32)
    return jnp.sum(jnp.where(chosen[..., None], product, 0.0), axis=2)


def spread_ranks(row_ranks, row_slots, held_first, held, rank, which):
    piece = row_ranks[:, :, which * rank : (which + 1) * rank]
    chosen = row_slots[:, :, None] == held_first + jnp.arange(held, dtype=jnp.int32)
    spread = jnp.where(chosen[..., None], piece[:, :, None, :], jnp.zeros((), BF16))
    return spread.reshape(piece.shape[0], piece.shape[1], held * rank)


def make_term(gathered, shrunk, row_slot, gate_weight, up_weight, expand_gate, expand_up):
    held = expand_gate.shape[0]
    rank = expand_gate.shape[1]
    width = expand_gate.shape[2]
    held_first = lax.axis_index("tk") * held
    stack_gate = expand_gate.reshape(held * rank, width)
    stack_up = expand_up.reshape(held * rank, width)

    def one(weight, stack, which):
        total = jnp.einsum("scd,df->csf", gathered, weight, preferred_element_type=F32)
        return total + jnp.einsum(
            "sch,hf->csf",
            spread_ranks(shrunk, row_slot, held_first, held, rank, which),
            stack,
            preferred_element_type=F32,
        )

    joined = jnp.concatenate(
        [one(gate_weight, stack_gate, 0), one(up_weight, stack_up, 1)], axis=2
    )
    return joined.reshape(gathered.shape[1], -1)


def on_any_mesh(
    hidden_in,
    gate_weight,
    up_weight,
    shrink_store,
    expand_gate,
    expand_up,
    block_adapter,
    store_slot,
):
    row_slot = slots_of_rows(block_adapter, store_slot)
    width = gate_weight.shape[1]
    gathered = lax.all_gather(hidden_in, "tm", axis=1, tiled=True)
    shrunk = lax.psum(
        shrink_part(gathered, row_slot, shrink_store), ("tm", "tk")
    ).astype(BF16)
    term = make_term(
        gathered, shrunk, row_slot, gate_weight, up_weight, expand_gate, expand_up
    )
    summed = lax.psum_scatter(term, "tk", scatter_dimension=0, tiled=True)
    pieces = summed.reshape(summed.shape[0], gathered.shape[0], 2, width)
    return (jax.nn.silu(pieces[:, :, 0, :]) * pieces[:, :, 1, :]).astype(BF16)


def swap_bits(value):
    return ((value & 1) << 1) | (value >> 1)


def block_slots(adapter_ref, slot_ref, group, steps, blocks):
    return [
        slot_ref[adapter_ref[step, group * blocks + block]]
        for step in range(steps)
        for block in range(blocks)
    ]


def assemble_kernel(own, one, two, three, shrink, rows_out, part_out):
    z = lax.axis_index("tm")
    t = lax.axis_index("tk")
    size = own.shape[0]
    for k, piece in enumerate((own, one, two, three)):
        place = swap_bits(z ^ t ^ k)
        rows_out[pl.ds(pl.multiple_of(place * size, size), size), :] = piece[...]
    part = jnp.dot(rows_out[...], shrink[...], preferred_element_type=F32)
    for place in range(4):
        group = t ^ swap_bits(place)
        part_out[pl.ds(pl.multiple_of(group * size, size), size), :] = part[
            place * size : (place + 1) * size
        ]


def assemble(pieces, shrink):
    rows = 4 * pieces[0].shape[0]
    depth, ranks = shrink.shape
    vmem = pl.BlockSpec(memory_space=pltpu.VMEM)
    return pl.pallas_call(
        assemble_kernel,
        in_specs=[vmem] * 5,
        out_specs=[vmem] * 2,
        out_shape=[
            jax.ShapeDtypeStruct((rows, depth), BF16),
            jax.ShapeDtypeStruct((rows, ranks), F32),
        ],
        compiler_params=pltpu.CompilerParams(vmem_limit_bytes=8 * MIB),
        cost_estimate=pl.CostEstimate(
            flops=2 * rows * depth * ranks, bytes_accessed=2 * MIB, transcendentals=0
        ),
        name="assemble_and_shrink",
    )(*pieces, shrink)


def spread_kernel(blocks, adapter_ref, slot_ref, first, second, out):
    t = lax.axis_index("tk")
    steps = adapter_ref.shape[0]
    size = first.shape[0] // 4
    parts = []
    for place in range(4):
        group = t ^ swap_bits(place)
        rows = pl.ds(pl.multiple_of(group * size, size), size)
        total = first[rows, :] + second[rows, :]
        slots = block_slots(adapter_ref, slot_ref, group, steps, blocks)
        for i, slot in enumerate(slots):
            here = total[i * BLOCK : (i + 1) * BLOCK]
            parts.append(jnp.where(slot == t, here, jnp.zeros_like(here)))
    out[...] = jnp.concatenate(parts, axis=0).astype(BF16)


def spread(first, second, block_adapter, store_slot):
    rows, ranks = first.shape
    blocks = block_adapter.shape[1] // 4
    vmem = pl.BlockSpec(memory_space=pltpu.VMEM)
    smem = pl.BlockSpec(memory_space=pltpu.SMEM)
    return pl.pallas_call(
        functools.partial(spread_kernel, blocks),
        in_specs=[smem, smem, vmem, vmem],
        out_specs=vmem,
        out_shape=jax.ShapeDtypeStruct((rows, ranks), BF16),
        compiler_params=pltpu.CompilerParams(vmem_limit_bytes=4 * MIB),
        cost_estimate=pl.CostEstimate(
            flops=2 * rows * ranks, bytes_accessed=rows * ranks * 10, transcendentals=0
        ),
        name="spread",
    )(block_adapter, store_slot, first, second)


def load_kernel(plan, *refs):
    sem = refs[-1]
    sources, targets = refs[: -1 - len(plan)], refs[-1 - len(plan) : -1]
    copies = []
    for i, (which, start, cols) in enumerate(plan):
        source = sources[which]
        source = source.at[0] if start is None else source.at[:, pl.ds(start, cols)]
        copies.append(pltpu.make_async_copy(source, targets[i], sem.at[i]))
    for copy in copies:
        copy.start()
    for copy in copies:
        copy.wait()


def load(plan, *arrays):
    shapes = [
        arrays[which].shape[1:] if start is None else (arrays[which].shape[0], cols)
        for which, start, cols in plan
    ]
    size = sum(2 * a * b for a, b in shapes)
    return pl.pallas_call(
        functools.partial(load_kernel, plan),
        in_specs=[pl.BlockSpec(memory_space=pltpu.HBM)] * len(arrays),
        out_specs=[pl.BlockSpec(memory_space=pltpu.VMEM)] * len(plan),
        out_shape=[pltpu.VMEM(shape, BF16) for shape in shapes],
        scratch_shapes=[pltpu.SemaphoreType.DMA((len(plan),))],
        compiler_params=pltpu.CompilerParams(vmem_limit_bytes=2 * MIB),
        cost_estimate=pl.CostEstimate(flops=0, bytes_accessed=2 * size, transcendentals=0),
        name="load",
    )(*[far(a) for a in arrays])


def product_kernel(
    start, cols, fetch, tile, x_ref, ranks_ref, gate, up, eg, eu, send, keep, buffer, sem
):
    rank = ranks_ref.shape[1] // 2
    rows = x_ref.shape[0]
    half, quarter = rows // 2, rows // 4

    def copy(j):
        return pltpu.make_async_copy(
            up.at[:, pl.ds(start + j * fetch, fetch)],
            buffer.at[:, pl.ds(j * fetch, fetch)],
            sem.at[j],
        )

    for j in range(cols // fetch):
        copy(j).start()
    for which in range(2):
        base = which * quarter
        for j in range(cols // tile):
            at = slice(j * tile, (j + 1) * tile)
            there = slice(start + j * tile, start + (j + 1) * tile)
            if which == 0:
                weight = gate[:, at]
            else:
                if j * tile % fetch == 0:
                    copy(j * tile // fetch).wait()
                weight = buffer[:, at]
            y = jnp.dot(x_ref[...], weight, preferred_element_type=F32)
            y += jnp.dot(
                ranks_ref[:, which * rank : (which + 1) * rank],
                (eg, eu)[which][:, there],
                preferred_element_type=F32,
            )
            keep[base : base + quarter, at] = y[quarter:half]
            keep[half + base : half + base + quarter, at] = y[:quarter]
            send[base : base + quarter, at] = y[half + quarter :].astype(BF16)
            send[half + base : half + base + quarter, at] = y[half : half + quarter].astype(BF16)


def product(x, ranks, gate, up, eg, eu, start, cols):
    rows, depth = x.shape
    fetch = 512 if cols % 512 == 0 else cols // 2
    vmem = pl.BlockSpec(memory_space=pltpu.VMEM)
    hbm = pl.BlockSpec(memory_space=pltpu.HBM)
    return pl.pallas_call(
        functools.partial(product_kernel, start, cols, fetch, TILE),
        in_specs=[vmem, vmem, vmem, hbm, vmem, vmem],
        out_specs=[vmem, vmem],
        out_shape=[
            pltpu.VMEM((rows, cols), BF16),
            pltpu.VMEM((rows, cols), F32),
        ],
        scratch_shapes=[
            pltpu.VMEM((depth, cols), BF16),
            pltpu.SemaphoreType.DMA((cols // fetch,)),
        ],
        compiler_params=pltpu.CompilerParams(vmem_limit_bytes=12 * MIB),
        cost_estimate=pl.CostEstimate(
            flops=4 * rows * depth * cols, bytes_accessed=4 * depth * cols, transcendentals=0
        ),
        name="product",
    )(x, ranks, near(gate), far(up), near(eg), near(eu))


def near(value):
    return pltpu.with_memory_space_constraint(value, pltpu.VMEM)


def far(value):
    return pltpu.with_memory_space_constraint(value, pltpu.HBM)


def on_pairs(
    hidden_in,
    gate_weight,
    up_weight,
    shrink_store,
    expand_gate,
    expand_up,
    block_adapter,
    store_slot,
):
    steps, here, depth = hidden_in.shape
    own = hidden_in.reshape(steps * here, depth)
    rows = 4 * steps * here

    def exchange(value, axis, bit):
        return lax.ppermute(value, axis, [(i, i ^ bit) for i in range(4)])

    three = exchange(own, "tm", 3)
    two = exchange(own, "tm", 2)
    one = exchange(own, "tm", 1)
    plan = [(0, None, None), (1, None, None), (2, None, None)]
    start = 0
    for cols in CHUNKS:
        plan.append((3, start, cols))
        start += cols
    shrink, eg, eu, *gates = load(
        tuple(plan), shrink_store, expand_gate, expand_up, gate_weight
    )
    x, part = assemble((own, one, two, three), shrink)

    pair = part + exchange(part, "tk", 1)

    def deliver(j):
        perm = []
        for a in range(4):
            for t in range(4):
                chip, core = t >> 1, t & 1
                perm.append((a * 4 + t, (2 * core + (chip ^ j)) * 4 + a))
        return lax.ppermute(pair, ("tm", "tk"), perm)

    ranks = spread(deliver(0), deliver(1), block_adapter, store_slot)

    half, quarter = rows // 2, rows // 4
    outs = []
    start = 0
    overs = []
    for j, cols in enumerate(CHUNKS):
        if j > 0:
            x, _ = lax.optimization_barrier((x, overs[max(j - 2, 0)]))
        send, keep = product(x, ranks, gates[j], up_weight, eg, eu, start, cols)
        got = exchange(send, "tk", 1)
        over = (keep[:half] + got[:half]).astype(BF16)
        overs.append(over)
        other = exchange(over, "tk", 2)
        total = keep[half:] + got[half:] + other
        gate, up = total[:quarter], total[quarter:]
        outs.append((jax.nn.silu(gate) * up).astype(BF16))
        start += cols
    out = jnp.concatenate(outs, axis=1).reshape(steps, here, -1)
    return jnp.transpose(out, (1, 0, 2))


def solution(mesh):
    paired = mesh.shape["tm"] == 4 and mesh.shape["tk"] == 4
    return jax.shard_map(
        on_pairs if paired else on_any_mesh,
        mesh=mesh,
        in_specs=(
            P(None, ("rep", "tm"), "tk"),
            P("tk", "tm"),
            P("tk", "tm"),
            P("tm", "tk", None),
            P("tk", None, "tm"),
            P("tk", None, "tm"),
            P(None, "rep"),
            P(),
        ),
        out_specs=P(("rep", "tk"), None, "tm"),
        check_vma=False,
    )
```

```python
import functools

import jax
import jax.numpy as jnp
from jax import lax
from jax.experimental import pallas as pl
from jax.experimental.pallas import tpu as pltpu
from jax.sharding import PartitionSpec as P

BLOCK = 8
MIB = 2**20
F32 = jnp.float32
BF16 = jnp.bfloat16
CHUNKS = (2048, 1536, 2048, 1536)
SLOTS = 5
FAT = 10**11
SPREAD = 10
PTIES = (("pair",), ("mine",), ())
TILE = 256


def slots_of_rows(block_adapter, store_slot):
    count = store_slot.shape[0]
    match = block_adapter[:, :, None] == jnp.arange(count, dtype=jnp.int32)
    block_slot = jnp.sum(jnp.where(match, store_slot, 0), axis=2)
    return jnp.repeat(block_slot, BLOCK, axis=1)


def shrink_part(gathered, row_slot, shrink_store):
    owned = shrink_store.shape[0]
    first = lax.axis_index("tm") * owned
    product = jnp.einsum(
        "srd,adk->srak", gathered, shrink_store, preferred_element_type=F32
    )
    chosen = row_slot[:, :, None] == first + jnp.arange(owned, dtype=jnp.int32)
    return jnp.sum(jnp.where(chosen[..., None], product, 0.0), axis=2)


def spread_ranks(row_ranks, row_slots, held_first, held, rank, which):
    piece = row_ranks[:, :, which * rank : (which + 1) * rank]
    chosen = row_slots[:, :, None] == held_first + jnp.arange(held, dtype=jnp.int32)
    spread = jnp.where(chosen[..., None], piece[:, :, None, :], jnp.zeros((), BF16))
    return spread.reshape(piece.shape[0], piece.shape[1], held * rank)


def make_term(gathered, shrunk, row_slot, gate_weight, up_weight, expand_gate, expand_up):
    held = expand_gate.shape[0]
    rank = expand_gate.shape[1]
    width = expand_gate.shape[2]
    held_first = lax.axis_index("tk") * held
    stack_gate = expand_gate.reshape(held * rank, width)
    stack_up = expand_up.reshape(held * rank, width)

    def one(weight, stack, which):
        total = jnp.einsum("scd,df->csf", gathered, weight, preferred_element_type=F32)
        return total + jnp.einsum(
            "sch,hf->csf",
            spread_ranks(shrunk, row_slot, held_first, held, rank, which),
            stack,
            preferred_element_type=F32,
        )

    joined = jnp.concatenate(
        [one(gate_weight, stack_gate, 0), one(up_weight, stack_up, 1)], axis=2
    )
    return joined.reshape(gathered.shape[1], -1)


def on_any_mesh(
    hidden_in,
    gate_weight,
    up_weight,
    shrink_store,
    expand_gate,
    expand_up,
    block_adapter,
    store_slot,
):
    row_slot = slots_of_rows(block_adapter, store_slot)
    width = gate_weight.shape[1]
    gathered = lax.all_gather(hidden_in, "tm", axis=1, tiled=True)
    shrunk = lax.psum(
        shrink_part(gathered, row_slot, shrink_store), ("tm", "tk")
    ).astype(BF16)
    term = make_term(
        gathered, shrunk, row_slot, gate_weight, up_weight, expand_gate, expand_up
    )
    summed = lax.psum_scatter(term, "tk", scatter_dimension=0, tiled=True)
    pieces = summed.reshape(summed.shape[0], gathered.shape[0], 2, width)
    return (jax.nn.silu(pieces[:, :, 0, :]) * pieces[:, :, 1, :]).astype(BF16)


def swap_bits(value):
    return ((value & 1) << 1) | (value >> 1)


def block_slots(adapter_ref, slot_ref, group, steps, blocks):
    return [
        slot_ref[adapter_ref[step, group * blocks + block]]
        for step in range(steps)
        for block in range(blocks)
    ]


def assemble_kernel(own, one, two, three, shrink, *refs):
    rows_out, part_out = refs[-2:]
    z = lax.axis_index("tm")
    t = lax.axis_index("tk")
    size = own.shape[0]
    for k, piece in enumerate((own, one, two, three)):
        place = swap_bits(z ^ t ^ k)
        rows_out[pl.ds(pl.multiple_of(place * size, size), size), :] = piece[...]
    part = jnp.dot(rows_out[...], shrink[...], preferred_element_type=F32)
    for place in range(4):
        group = t ^ swap_bits(place)
        part_out[pl.ds(pl.multiple_of(group * size, size), size), :] = part[
            place * size : (place + 1) * size
        ]


def assemble(pieces, shrink, ties):
    rows = 4 * pieces[0].shape[0]
    depth, ranks = shrink.shape
    vmem = pl.BlockSpec(memory_space=pltpu.VMEM)
    return pl.pallas_call(
        assemble_kernel,
        in_specs=[vmem] * 5 + [pl.BlockSpec(memory_space=pl.ANY)] * len(ties),
        out_specs=[vmem] * 2,
        out_shape=[
            jax.ShapeDtypeStruct((rows, depth), BF16),
            jax.ShapeDtypeStruct((rows, ranks), F32),
        ],
        compiler_params=pltpu.CompilerParams(vmem_limit_bytes=8 * MIB),
        cost_estimate=pl.CostEstimate(
            flops=2 * rows * depth * ranks, bytes_accessed=2 * MIB, transcendentals=0
        ),
        name="assemble_and_shrink",
    )(*pieces, shrink, *ties)


def spread_kernel(blocks, adapter_ref, slot_ref, mine, theirs, out):
    t = lax.axis_index("tk")
    steps = adapter_ref.shape[0]
    size = mine.shape[0] // 4
    rank = mine.shape[1] // 2
    parts = []
    for place in (1, 0):
        group = t ^ swap_bits(place)
        rows = pl.ds(pl.multiple_of(group * size, size), size)
        pair = [ref[rows, :].astype(F32) for ref in (mine, theirs)]
        slots = block_slots(adapter_ref, slot_ref, group, steps, blocks)
        for i, slot in enumerate(slots):
            here = []
            for held, value in ((t, pair[0]), (t ^ 1, pair[1])):
                block = value[i * BLOCK : (i + 1) * BLOCK]
                here.append(jnp.where(slot == held, block, jnp.zeros_like(block)))
            parts.append(
                jnp.concatenate(
                    [
                        here[0][:, :rank],
                        here[1][:, :rank],
                        here[0][:, rank:],
                        here[1][:, rank:],
                    ],
                    axis=1,
                )
            )
    out[...] = jnp.concatenate(parts, axis=0).astype(BF16)


def spread(mine, theirs, block_adapter, store_slot):
    rows, ranks = mine.shape
    blocks = block_adapter.shape[1] // 4
    vmem = pl.BlockSpec(memory_space=pltpu.VMEM)
    smem = pl.BlockSpec(memory_space=pltpu.SMEM)
    return pl.pallas_call(
        functools.partial(spread_kernel, blocks),
        in_specs=[smem, smem, vmem, vmem],
        out_specs=vmem,
        out_shape=jax.ShapeDtypeStruct((rows // 2, 2 * ranks), BF16),
        compiler_params=pltpu.CompilerParams(vmem_limit_bytes=4 * MIB),
        cost_estimate=pl.CostEstimate(flops=SPREAD, bytes_accessed=SPREAD // 1000, transcendentals=0),
        name="spread",
    )(block_adapter, store_slot, mine, theirs)


def over_kernel(start, tile, ranks_ref, eg, eu, fg, fu, keep, got, *refs):
    over, own = refs[-2:]
    cols = keep.shape[1]
    half = keep.shape[0] // 2
    quarter = half // 2
    wide = ranks_ref.shape[1] // 2
    for j in range(cols // tile):
        at = slice(j * tile, (j + 1) * tile)
        there = slice(start + j * tile, start + (j + 1) * tile)
        for which, (mine, theirs) in enumerate(((eg, fg), (eu, fu))):
            expand = jnp.concatenate([mine[:, there], theirs[:, there]], axis=0)
            y = jnp.dot(
                ranks_ref[:, which * wide : (which + 1) * wide],
                expand,
                preferred_element_type=F32,
            )
            far_rows = slice(which * quarter, (which + 1) * quarter)
            own_rows = slice(half + which * quarter, half + (which + 1) * quarter)
            over[far_rows, at] = (
                keep[far_rows, at] + got[far_rows, at].astype(F32) + y[:quarter]
            ).astype(BF16)
            own[far_rows, at] = (
                keep[own_rows, at] + got[own_rows, at].astype(F32) + y[quarter:]
            )


def pair_sum(ranks, expands, keep, got, start, ties):
    rows, cols = keep.shape
    vmem = pl.BlockSpec(memory_space=pltpu.VMEM)
    return pl.pallas_call(
        functools.partial(over_kernel, start, TILE),
        in_specs=[vmem] * 7 + [pl.BlockSpec(memory_space=pl.ANY)] * len(ties),
        out_specs=[vmem] * 2,
        out_shape=[
            pltpu.VMEM((rows // 2, cols), BF16),
            pltpu.VMEM((rows // 2, cols), F32),
        ],
        compiler_params=pltpu.CompilerParams(vmem_limit_bytes=4 * MIB),
        cost_estimate=pl.CostEstimate(
            flops=1,
            bytes_accessed=1,
            transcendentals=0,
        ),
        name="pair_sum",
    )(ranks, *[near(e) for e in expands], keep, got, *ties)


def finish_kernel(start, tile, own, other, before, *refs):
    del before
    out, block, sem = refs[-3:]
    cols = own.shape[1]
    quarter = own.shape[0] // 2
    here = quarter // 2
    for j in range(cols // tile):
        at = slice(j * tile, (j + 1) * tile)
        total = own[:, at] + other[:, at].astype(F32)
        gate, up = total[:quarter], total[quarter:]
        done = (gate / (1.0 + jnp.exp(-gate)) * up).astype(BF16)
        for step in range(quarter // here):
            block[:, step, at] = done[step * here : (step + 1) * here]
    copy = pltpu.make_async_copy(block, out.at[:, :, pl.ds(start, cols)], sem)
    copy.start()
    copy.wait()


def finish(own, other, before, start, ties):
    half, cols = own.shape
    shape = before.shape
    vmem = pl.BlockSpec(memory_space=pltpu.VMEM)
    hbm = pl.BlockSpec(memory_space=pltpu.HBM)
    return pl.pallas_call(
        functools.partial(finish_kernel, start, TILE),
        in_specs=[vmem, vmem, hbm] + [pl.BlockSpec(memory_space=pl.ANY)] * len(ties),
        out_specs=hbm,
        out_shape=jax.ShapeDtypeStruct(shape, BF16),
        input_output_aliases={2: 0},
        scratch_shapes=[
            pltpu.VMEM((shape[0], shape[1], cols), BF16),
            pltpu.SemaphoreType.DMA(()),
        ],
        compiler_params=pltpu.CompilerParams(vmem_limit_bytes=4 * MIB),
        cost_estimate=pl.CostEstimate(
            flops=1, bytes_accessed=1, transcendentals=0
        ),
        name="finish",
    )(own, other, before, *ties)


def join_kernel(first, second, out):
    out[...] = (first[...] + second[...]).astype(BF16)


def join(first, second):
    vmem = pl.BlockSpec(memory_space=pltpu.VMEM)
    return pl.pallas_call(
        join_kernel,
        in_specs=[vmem] * 2,
        out_specs=vmem,
        out_shape=jax.ShapeDtypeStruct(first.shape, BF16),
        compiler_params=pltpu.CompilerParams(vmem_limit_bytes=2 * MIB),
        cost_estimate=pl.CostEstimate(flops=FAT, bytes_accessed=FAT // 1000, transcendentals=0),
        name="join",
    )(first, second)


def after_kernel(*refs):
    out = refs[-1]
    out[...] = jnp.zeros_like(out)


def after(*values):
    return pl.pallas_call(
        after_kernel,
        in_specs=[pl.BlockSpec(memory_space=pl.ANY)] * len(values),
        out_specs=pl.BlockSpec(memory_space=pltpu.VMEM),
        out_shape=jax.ShapeDtypeStruct((8, 128), F32),
        compiler_params=pltpu.CompilerParams(vmem_limit_bytes=2 * MIB),
        cost_estimate=pl.CostEstimate(flops=FAT, bytes_accessed=FAT // 1000, transcendentals=0),
        name="after",
    )(*values)


def blank_kernel(out):
    del out


def blank(shape):
    return pl.pallas_call(
        blank_kernel,
        out_specs=pl.BlockSpec(memory_space=pltpu.HBM),
        out_shape=jax.ShapeDtypeStruct(shape, BF16),
        compiler_params=pltpu.CompilerParams(vmem_limit_bytes=2 * MIB),
        name="blank",
    )()


def load_kernel(plan, *refs):
    sem = refs[-1]
    sources, targets = refs[: -1 - len(plan)], refs[-1 - len(plan) : -1]
    copies = []
    for i, (which, start, cols) in enumerate(plan):
        source = sources[which]
        source = source.at[0] if start is None else source.at[:, pl.ds(start, cols)]
        copies.append(pltpu.make_async_copy(source, targets[i], sem.at[i]))
    for copy in copies:
        copy.start()
    for copy in copies:
        copy.wait()


def load(plan, *arrays):
    shapes = [
        arrays[which].shape[1:] if start is None else (arrays[which].shape[0], cols)
        for which, start, cols in plan
    ]
    size = sum(2 * a * b for a, b in shapes)
    return pl.pallas_call(
        functools.partial(load_kernel, plan),
        in_specs=[pl.BlockSpec(memory_space=pltpu.HBM)] * len(arrays),
        out_specs=[pl.BlockSpec(memory_space=pltpu.VMEM)] * len(plan),
        out_shape=[pltpu.VMEM(shape, BF16) for shape in shapes],
        scratch_shapes=[pltpu.SemaphoreType.DMA((len(plan),))],
        compiler_params=pltpu.CompilerParams(vmem_limit_bytes=2 * MIB),
        cost_estimate=pl.CostEstimate(flops=0, bytes_accessed=2 * size, transcendentals=0),
        name="load",
    )(*[far(a) for a in arrays])


def product_kernel(start, fetch, tile, ties, x_ref, gate, up, *refs):
    send, keep, buffer, sem = refs[ties:]
    rows, cols = keep.shape
    half, quarter = rows // 2, rows // 4
    slots = buffer.shape[0]
    count = cols // fetch

    def copy(j):
        return pltpu.make_async_copy(
            up.at[:, pl.ds(start + j * fetch, fetch)],
            buffer.at[j % slots],
            sem.at[j % slots],
        )

    def multiply(which, weight, at):
        base = which * quarter
        y = jnp.dot(x_ref[...], weight, preferred_element_type=F32)
        keep[base : base + quarter, at] = y[quarter:half]
        keep[half + base : half + base + quarter, at] = y[:quarter]
        send[base : base + quarter, at] = y[half + quarter :].astype(BF16)
        send[half + base : half + base + quarter, at] = y[half : half + quarter].astype(BF16)

    for j in range(min(slots, count)):
        copy(j).start()
    for j in range(count):
        places = [slice(j * fetch + k, j * fetch + k + tile) for k in range(0, fetch, tile)]
        for at in places:
            multiply(0, gate[:, at], at)
        copy(j).wait()
        for k, at in enumerate(places):
            multiply(1, buffer[j % slots, :, k * tile : (k + 1) * tile], at)
        if j + slots < count:
            copy(j + slots).start()


def product(x, gate, up, start, cols, ties):
    rows, depth = x.shape
    fetch = 512
    slots = min(SLOTS, cols // fetch)
    vmem = pl.BlockSpec(memory_space=pltpu.VMEM)
    hbm = pl.BlockSpec(memory_space=pltpu.HBM)
    return pl.pallas_call(
        functools.partial(product_kernel, start, fetch, TILE, len(ties)),
        in_specs=[vmem, vmem, hbm] + [pl.BlockSpec(memory_space=pl.ANY)] * len(ties),
        out_specs=[vmem, vmem],
        out_shape=[
            pltpu.VMEM((rows, cols), BF16),
            pltpu.VMEM((rows, cols), F32),
        ],
        scratch_shapes=[
            pltpu.VMEM((slots, depth, fetch), BF16),
            pltpu.SemaphoreType.DMA((slots,)),
        ],
        compiler_params=pltpu.CompilerParams(vmem_limit_bytes=14 * MIB),
        cost_estimate=pl.CostEstimate(
            flops=1, bytes_accessed=1, transcendentals=0
        ),
        name="product",
    )(x, near(gate), far(up), *ties)


def near(value):
    return pltpu.with_memory_space_constraint(value, pltpu.VMEM)


def far(value):
    return pltpu.with_memory_space_constraint(value, pltpu.HBM)


def on_pairs(
    hidden_in,
    gate_weight,
    up_weight,
    shrink_store,
    expand_gate,
    expand_up,
    block_adapter,
    store_slot,
):
    steps, here, depth = hidden_in.shape
    held = hidden_in.reshape(steps * here, depth)
    rows = 4 * steps * here

    def exchange(value, axis, bit):
        return lax.ppermute(value, axis, [(i, i ^ bit) for i in range(4)])

    fg = exchange(expand_gate[0], "tk", 1)
    fu = exchange(expand_up[0], "tk", 1)
    three = exchange(held, "tm", 3)
    two = exchange(held, "tm", 2)
    one = exchange(held, "tm", 1)
    plan = [(0, None, None), (1, None, None), (2, None, None)]
    start = 0
    for cols in CHUNKS:
        plan.append((3, start, cols))
        start += cols
    shrink, eg, eu, *gates = load(
        tuple(plan), shrink_store, expand_gate, expand_up, gate_weight
    )
    x, part = assemble((held, one, two, three), shrink, (fg, fu))

    pair = part + exchange(part, "tk", 1)

    def deliver(j):
        perm = []
        for a in range(4):
            for t in range(4):
                chip, core = t >> 1, t & 1
                perm.append((a * 4 + t, (2 * core + (chip ^ j)) * 4 + a))
        return lax.ppermute(pair, ("tm", "tk"), perm)

    mine = join(deliver(0), deliver(1))

    theirs = exchange(mine, "tk", 1)
    ranks = spread(mine, theirs, block_adapter, store_slot)
    out = blank((here, steps, sum(CHUNKS)))

    overs, owns, others, sends = [], [], [], []
    start = 0
    for j, cols in enumerate(CHUNKS):
        ties = ((pair,), (mine, *sends[:1]), overs[:2], sends[2:3])[j]
        send, keep = product(x, gates[j], up_weight, start, cols, ties)
        sends.append(send)
        got = exchange(send, "tk", 1)
        ties = ((), overs[:1], (after(*others),) if j == 2 else (), overs[2:3])[j]
        over, own = pair_sum(ranks, (eg, eu, fg, fu), keep, got, start, ties)
        overs.append(over)
        owns.append(own)
        others.append(exchange(over, "tk", 2))
        start += cols
    start = 0
    for j, cols in enumerate(CHUNKS):
        out = finish(owns[j], others[j], out, start, overs[-1:])
        start += cols
    return out


def solution(mesh):
    paired = mesh.shape["tm"] == 4 and mesh.shape["tk"] == 4
    return jax.shard_map(
        on_pairs if paired else on_any_mesh,
        mesh=mesh,
        in_specs=(
            P(None, ("rep", "tm"), "tk"),
            P("tk", "tm"),
            P("tk", "tm"),
            P("tm", "tk", None),
            P("tk", None, "tm"),
            P("tk", None, "tm"),
            P(None, "rep"),
            P(),
        ),
        out_specs=P(("rep", "tk"), None, "tm"),
        check_vma=False,
    )
```

```python
import functools

import jax
import jax.numpy as jnp
from jax import lax
from jax.experimental import pallas as pl
from jax.experimental.pallas import tpu as pltpu
from jax.sharding import PartitionSpec as P

BLOCK = 8
MIB = 2**20
F32 = jnp.float32
BF16 = jnp.bfloat16
CHUNKS = (2048, 1536, 2048, 1536)
SLOTS = 5
LEAD = 2
FAT = 10**11
SPREAD = 10**11
PTIES = (("pair",), ("mine",), ())
TILE = 256


def slots_of_rows(block_adapter, store_slot):
    count = store_slot.shape[0]
    match = block_adapter[:, :, None] == jnp.arange(count, dtype=jnp.int32)
    block_slot = jnp.sum(jnp.where(match, store_slot, 0), axis=2)
    return jnp.repeat(block_slot, BLOCK, axis=1)


def shrink_part(gathered, row_slot, shrink_store):
    owned = shrink_store.shape[0]
    first = lax.axis_index("tm") * owned
    product = jnp.einsum(
        "srd,adk->srak", gathered, shrink_store, preferred_element_type=F32
    )
    chosen = row_slot[:, :, None] == first + jnp.arange(owned, dtype=jnp.int32)
    return jnp.sum(jnp.where(chosen[..., None], product, 0.0), axis=2)


def spread_ranks(row_ranks, row_slots, held_first, held, rank, which):
    piece = row_ranks[:, :, which * rank : (which + 1) * rank]
    chosen = row_slots[:, :, None] == held_first + jnp.arange(held, dtype=jnp.int32)
    spread = jnp.where(chosen[..., None], piece[:, :, None, :], jnp.zeros((), BF16))
    return spread.reshape(piece.shape[0], piece.shape[1], held * rank)


def make_term(gathered, shrunk, row_slot, gate_weight, up_weight, expand_gate, expand_up):
    held = expand_gate.shape[0]
    rank = expand_gate.shape[1]
    width = expand_gate.shape[2]
    held_first = lax.axis_index("tk") * held
    stack_gate = expand_gate.reshape(held * rank, width)
    stack_up = expand_up.reshape(held * rank, width)

    def one(weight, stack, which):
        total = jnp.einsum("scd,df->csf", gathered, weight, preferred_element_type=F32)
        return total + jnp.einsum(
            "sch,hf->csf",
            spread_ranks(shrunk, row_slot, held_first, held, rank, which),
            stack,
            preferred_element_type=F32,
        )

    joined = jnp.concatenate(
        [one(gate_weight, stack_gate, 0), one(up_weight, stack_up, 1)], axis=2
    )
    return joined.reshape(gathered.shape[1], -1)


def on_any_mesh(
    hidden_in,
    gate_weight,
    up_weight,
    shrink_store,
    expand_gate,
    expand_up,
    block_adapter,
    store_slot,
):
    row_slot = slots_of_rows(block_adapter, store_slot)
    width = gate_weight.shape[1]
    gathered = lax.all_gather(hidden_in, "tm", axis=1, tiled=True)
    shrunk = lax.psum(
        shrink_part(gathered, row_slot, shrink_store), ("tm", "tk")
    ).astype(BF16)
    term = make_term(
        gathered, shrunk, row_slot, gate_weight, up_weight, expand_gate, expand_up
    )
    summed = lax.psum_scatter(term, "tk", scatter_dimension=0, tiled=True)
    pieces = summed.reshape(summed.shape[0], gathered.shape[0], 2, width)
    return (jax.nn.silu(pieces[:, :, 0, :]) * pieces[:, :, 1, :]).astype(BF16)


def swap_bits(value):
    return ((value & 1) << 1) | (value >> 1)


def block_slots(adapter_ref, slot_ref, group, steps, blocks):
    return [
        slot_ref[adapter_ref[step, group * blocks + block]]
        for step in range(steps)
        for block in range(blocks)
    ]


def assemble_kernel(own, one, two, three, shrink, *refs):
    rows_out, part_out = refs[-2:]
    z = lax.axis_index("tm")
    t = lax.axis_index("tk")
    size = own.shape[0]
    for k, piece in enumerate((own, one, two, three)):
        place = swap_bits(z ^ t ^ k)
        rows_out[pl.ds(pl.multiple_of(place * size, size), size), :] = piece[...]
    part = jnp.dot(rows_out[...], shrink[...], preferred_element_type=F32)
    for place in range(4):
        group = t ^ swap_bits(place)
        part_out[pl.ds(pl.multiple_of(group * size, size), size), :] = part[
            place * size : (place + 1) * size
        ]


def assemble(pieces, shrink, ties):
    rows = 4 * pieces[0].shape[0]
    depth, ranks = shrink.shape
    vmem = pl.BlockSpec(memory_space=pltpu.VMEM)
    return pl.pallas_call(
        assemble_kernel,
        in_specs=[vmem] * 5 + [pl.BlockSpec(memory_space=pl.ANY)] * len(ties),
        out_specs=[vmem] * 2,
        out_shape=[
            jax.ShapeDtypeStruct((rows, depth), BF16),
            jax.ShapeDtypeStruct((rows, ranks), F32),
        ],
        compiler_params=pltpu.CompilerParams(vmem_limit_bytes=8 * MIB),
        cost_estimate=pl.CostEstimate(
            flops=2 * rows * depth * ranks, bytes_accessed=2 * MIB, transcendentals=0
        ),
        name="assemble_and_shrink",
    )(*pieces, shrink, *ties)


def spread_kernel(mask, mine, theirs, out):
    t = lax.axis_index("tk")
    size = mine.shape[0] // 4
    rank = mine.shape[1] // 2
    for half, place in enumerate((1, 0)):
        group = t ^ swap_bits(place)
        rows = pl.ds(pl.multiple_of(group * size, size), size)
        here = []
        for i, ref in enumerate((mine, theirs)):
            value = ref[rows, :].astype(F32)
            chosen = mask[i, half * size : (half + 1) * size, :] > 0.5
            here.append(jnp.where(chosen, value, jnp.zeros_like(value)))
        out[half * size : (half + 1) * size, :] = jnp.concatenate(
            [here[0][:, :rank], here[1][:, :rank], here[0][:, rank:], here[1][:, rank:]], axis=1
        ).astype(BF16)


def spread(mask, mine, theirs):
    rows, ranks = mine.shape
    vmem = pl.BlockSpec(memory_space=pltpu.VMEM)
    return pl.pallas_call(
        spread_kernel,
        in_specs=[vmem] * 3,
        out_specs=vmem,
        out_shape=jax.ShapeDtypeStruct((rows // 2, 2 * ranks), BF16),
        compiler_params=pltpu.CompilerParams(vmem_limit_bytes=2 * MIB),
        cost_estimate=pl.CostEstimate(flops=SPREAD, bytes_accessed=SPREAD // 1000, transcendentals=0),
        name="spread",
    )(mask, mine, theirs)


def over_kernel(start, tile, ranks_ref, eg, eu, fg, fu, keep, got, *refs):
    over, own = refs[-2:]
    cols = keep.shape[1]
    half = keep.shape[0] // 2
    quarter = half // 2
    wide = ranks_ref.shape[1] // 2
    for j in range(cols // tile):
        at = slice(j * tile, (j + 1) * tile)
        there = slice(start + j * tile, start + (j + 1) * tile)
        for which, (mine, theirs) in enumerate(((eg, fg), (eu, fu))):
            expand = jnp.concatenate([mine[:, there], theirs[:, there]], axis=0)
            y = jnp.dot(
                ranks_ref[:, which * wide : (which + 1) * wide],
                expand,
                preferred_element_type=F32,
            )
            far_rows = slice(which * quarter, (which + 1) * quarter)
            own_rows = slice(half + which * quarter, half + (which + 1) * quarter)
            over[far_rows, at] = (
                keep[far_rows, at] + got[far_rows, at].astype(F32) + y[:quarter]
            ).astype(BF16)
            own[far_rows, at] = (
                keep[own_rows, at] + got[own_rows, at].astype(F32) + y[quarter:]
            )


def pair_sum(ranks, expands, keep, got, start, ties):
    rows, cols = keep.shape
    vmem = pl.BlockSpec(memory_space=pltpu.VMEM)
    return pl.pallas_call(
        functools.partial(over_kernel, start, TILE),
        in_specs=[vmem] * 7 + [pl.BlockSpec(memory_space=pl.ANY)] * len(ties),
        out_specs=[vmem] * 2,
        out_shape=[
            pltpu.VMEM((rows // 2, cols), BF16),
            pltpu.VMEM((rows // 2, cols), F32),
        ],
        compiler_params=pltpu.CompilerParams(vmem_limit_bytes=4 * MIB),
        cost_estimate=pl.CostEstimate(
            flops=1,
            bytes_accessed=1,
            transcendentals=0,
        ),
        name="pair_sum",
    )(ranks, *[near(e) for e in expands], keep, got, *ties)


def finish_kernel(start, tile, own, other, before, *refs):
    del before
    out, block, sem = refs[-3:]
    cols = own.shape[1]
    quarter = own.shape[0] // 2
    here = quarter // 2
    for j in range(cols // tile):
        at = slice(j * tile, (j + 1) * tile)
        total = own[:, at] + other[:, at].astype(F32)
        gate, up = total[:quarter], total[quarter:]
        done = (gate / (1.0 + jnp.exp(-gate)) * up).astype(BF16)
        for step in range(quarter // here):
            block[:, step, at] = done[step * here : (step + 1) * here]
    copy = pltpu.make_async_copy(block, out.at[:, :, pl.ds(start, cols)], sem)
    copy.start()
    copy.wait()


def finish(own, other, before, start, ties):
    half, cols = own.shape
    shape = before.shape
    vmem = pl.BlockSpec(memory_space=pltpu.VMEM)
    hbm = pl.BlockSpec(memory_space=pltpu.HBM)
    return pl.pallas_call(
        functools.partial(finish_kernel, start, TILE),
        in_specs=[vmem, vmem, hbm] + [pl.BlockSpec(memory_space=pl.ANY)] * len(ties),
        out_specs=hbm,
        out_shape=jax.ShapeDtypeStruct(shape, BF16),
        input_output_aliases={2: 0},
        scratch_shapes=[
            pltpu.VMEM((shape[0], shape[1], cols), BF16),
            pltpu.SemaphoreType.DMA(()),
        ],
        compiler_params=pltpu.CompilerParams(vmem_limit_bytes=4 * MIB),
        cost_estimate=pl.CostEstimate(
            flops=1, bytes_accessed=1, transcendentals=0
        ),
        name="finish",
    )(own, other, before, *ties)


def join_kernel(first, second, *refs):
    out = refs[-1]
    out[...] = (first[...] + second[...]).astype(out.dtype)


def join(first, second, dtype, ties):
    vmem = pl.BlockSpec(memory_space=pltpu.VMEM)
    return pl.pallas_call(
        join_kernel,
        in_specs=[vmem] * 2 + [pl.BlockSpec(memory_space=pl.ANY)] * len(ties),
        out_specs=vmem,
        out_shape=jax.ShapeDtypeStruct(first.shape, dtype),
        compiler_params=pltpu.CompilerParams(vmem_limit_bytes=2 * MIB),
        cost_estimate=pl.CostEstimate(flops=FAT, bytes_accessed=FAT // 1000, transcendentals=0),
        name="join",
    )(first, second, *ties)


def after_kernel(*refs):
    out = refs[-1]
    out[...] = jnp.zeros_like(out)


def after(*values):
    return pl.pallas_call(
        after_kernel,
        in_specs=[pl.BlockSpec(memory_space=pl.ANY)] * len(values),
        out_specs=pl.BlockSpec(memory_space=pltpu.VMEM),
        out_shape=jax.ShapeDtypeStruct((8, 128), F32),
        compiler_params=pltpu.CompilerParams(vmem_limit_bytes=2 * MIB),
        cost_estimate=pl.CostEstimate(flops=FAT, bytes_accessed=FAT // 1000, transcendentals=0),
        name="after",
    )(*values)


def blank_kernel(out):
    del out


def blank(shape):
    return pl.pallas_call(
        blank_kernel,
        out_specs=pl.BlockSpec(memory_space=pltpu.HBM),
        out_shape=jax.ShapeDtypeStruct(shape, BF16),
        compiler_params=pltpu.CompilerParams(vmem_limit_bytes=2 * MIB),
        name="blank",
    )()


def load_kernel(plan, *refs):
    sem = refs[-1]
    sources, targets = refs[: -1 - len(plan)], refs[-1 - len(plan) : -1]
    copies = []
    for i, (which, start, cols) in enumerate(plan):
        source = sources[which]
        source = source.at[0] if start is None else source.at[:, pl.ds(start, cols)]
        copies.append(pltpu.make_async_copy(source, targets[i], sem.at[i]))
    for copy in copies:
        copy.start()
    for copy in copies:
        copy.wait()


def load(plan, *arrays):
    shapes = [
        arrays[which].shape[1:] if start is None else (arrays[which].shape[0], cols)
        for which, start, cols in plan
    ]
    size = sum(2 * a * b for a, b in shapes)
    return pl.pallas_call(
        functools.partial(load_kernel, plan),
        in_specs=[pl.BlockSpec(memory_space=pltpu.HBM)] * len(arrays),
        out_specs=[pl.BlockSpec(memory_space=pltpu.VMEM)] * len(plan),
        out_shape=[pltpu.VMEM(shape, BF16) for shape in shapes],
        scratch_shapes=[pltpu.SemaphoreType.DMA((len(plan),))],
        compiler_params=pltpu.CompilerParams(vmem_limit_bytes=2 * MIB),
        cost_estimate=pl.CostEstimate(flops=0, bytes_accessed=2 * size, transcendentals=0),
        name="load",
    )(*[far(a) for a in arrays])


def mask_kernel(blocks, adapter_ref, slot_ref, mask):
    t = lax.axis_index("tk")
    row = 0
    for place in (1, 0):
        group = t ^ swap_bits(place)
        slots = block_slots(adapter_ref, slot_ref, group, adapter_ref.shape[0], blocks)
        for slot in slots:
            for i, held in enumerate((t, t ^ 1)):
                value = jnp.where(slot == held, 1.0, 0.0)
                mask[i, row : row + BLOCK, :] = jnp.full((BLOCK, mask.shape[2]), value, F32)
            row += BLOCK


def masks(block_adapter, store_slot, ranks):
    blocks = block_adapter.shape[1] // 4
    rows = 2 * block_adapter.shape[0] * blocks * BLOCK
    return pl.pallas_call(
        functools.partial(mask_kernel, blocks),
        in_specs=[pl.BlockSpec(memory_space=pltpu.SMEM)] * 2,
        out_specs=pl.BlockSpec(memory_space=pltpu.VMEM),
        out_shape=jax.ShapeDtypeStruct((2, rows, ranks), F32),
        compiler_params=pltpu.CompilerParams(vmem_limit_bytes=2 * MIB),
        cost_estimate=pl.CostEstimate(flops=1, bytes_accessed=1, transcendentals=0),
        name="masks",
    )(block_adapter, store_slot)


def product_kernel(start, fetch, tile, ties, x_ref, gate, up, *refs):
    send, keep, buffer, sem = refs[ties:]
    rows, cols = keep.shape
    half, quarter = rows // 2, rows // 4
    slots = buffer.shape[0]
    count = cols // fetch

    def copy(j):
        return pltpu.make_async_copy(
            up.at[:, pl.ds(start + j * fetch, fetch)],
            buffer.at[j % slots],
            sem.at[j % slots],
        )

    def multiply(which, j):
        base = which * quarter
        for k in range(0, fetch, tile):
            at = slice(j * fetch + k, j * fetch + k + tile)
            if which == 0:
                weight = gate[:, at]
            else:
                weight = buffer[j % slots, :, k : k + tile]
            y = jnp.dot(x_ref[...], weight, preferred_element_type=F32)
            keep[base : base + quarter, at] = y[quarter:half]
            keep[half + base : half + base + quarter, at] = y[:quarter]
            send[base : base + quarter, at] = y[half + quarter :].astype(BF16)
            send[half + base : half + base + quarter, at] = y[half : half + quarter].astype(BF16)

    for j in range(min(slots, count)):
        copy(j).start()
    lead = min(LEAD, count)
    for j in range(lead):
        multiply(0, j)
    for j in range(count):
        copy(j).wait()
        multiply(1, j)
        if j + slots < count:
            copy(j + slots).start()
        if j + lead < count:
            multiply(0, j + lead)


def product(x, gate, up, start, cols, ties):
    rows, depth = x.shape
    fetch = 512
    slots = min(SLOTS, cols // fetch)
    vmem = pl.BlockSpec(memory_space=pltpu.VMEM)
    hbm = pl.BlockSpec(memory_space=pltpu.HBM)
    return pl.pallas_call(
        functools.partial(product_kernel, start, fetch, TILE, len(ties)),
        in_specs=[vmem, vmem, hbm] + [pl.BlockSpec(memory_space=pl.ANY)] * len(ties),
        out_specs=[vmem, vmem],
        out_shape=[
            pltpu.VMEM((rows, cols), BF16),
            pltpu.VMEM((rows, cols), F32),
        ],
        scratch_shapes=[
            pltpu.VMEM((slots, depth, fetch), BF16),
            pltpu.SemaphoreType.DMA((slots,)),
        ],
        compiler_params=pltpu.CompilerParams(vmem_limit_bytes=14 * MIB),
        cost_estimate=pl.CostEstimate(flops=1, bytes_accessed=1, transcendentals=0),
        name="product",
    )(x, near(gate), far(up), *ties)


def near(value):
    return pltpu.with_memory_space_constraint(value, pltpu.VMEM)


def far(value):
    return pltpu.with_memory_space_constraint(value, pltpu.HBM)


def on_pairs(
    hidden_in,
    gate_weight,
    up_weight,
    shrink_store,
    expand_gate,
    expand_up,
    block_adapter,
    store_slot,
):
    steps, here, depth = hidden_in.shape
    held = hidden_in.reshape(steps * here, depth)
    rows = 4 * steps * here

    def exchange(value, axis, bit):
        return lax.ppermute(value, axis, [(i, i ^ bit) for i in range(4)])

    fg = exchange(expand_gate[0], "tk", 1)
    fu = exchange(expand_up[0], "tk", 1)
    three = exchange(held, "tm", 3)
    two = exchange(held, "tm", 2)
    one = exchange(held, "tm", 1)
    plan = [(0, None, None), (1, None, None), (2, None, None)]
    starts = [sum(CHUNKS[:j]) for j in range(len(CHUNKS))]
    for start, cols in zip(starts, CHUNKS):
        plan.append((3, start, cols))
    shrink, eg, eu, *gates = load(
        tuple(plan), shrink_store, expand_gate, expand_up, gate_weight
    )
    x, part = assemble((held, one, two, three), shrink, (fg, fu))
    mask = masks(block_adapter, store_slot, shrink_store.shape[2])
    pair = join(part, exchange(part, "tk", 1), F32, (mask,))

    def deliver(j):
        perm = []
        for a in range(4):
            for t in range(4):
                chip, core = t >> 1, t & 1
                perm.append((a * 4 + t, (2 * core + (chip ^ j)) * 4 + a))
        return lax.ppermute(pair, ("tm", "tk"), perm)

    sends, keeps, gots = [], [], []
    overs, owns, others = [], [], []

    def multiply(j, ties):
        send, keep = product(
            x, gates[j], up_weight, starts[j], CHUNKS[j], ties
        )
        sends.append(send)
        keeps.append(keep)
        gots.append(exchange(send, "tk", 1))

    def add_pair(j, ties):
        over, own = pair_sum(
            ranks, (eg, eu, fg, fu), keeps[j], gots[j], starts[j], ties
        )
        overs.append(over)
        owns.append(own)
        others.append(exchange(over, "tk", 2))

    multiply(0, (pair,))
    mine = join(deliver(0), deliver(1), BF16, (sends[0],))
    theirs = exchange(mine, "tk", 1)
    multiply(1, (mine,))
    ranks = spread(mask, mine, theirs)
    add_pair(0, (sends[1],))
    add_pair(1, (overs[0],))
    multiply(2, (overs[0], overs[1]))
    multiply(3, (sends[2],))
    add_pair(2, (after(others[0], others[1]),))
    add_pair(3, (overs[2],))
    out = blank((here, steps, sum(CHUNKS)))
    for j in range(len(CHUNKS)):
        out = finish(owns[j], others[j], out, starts[j], overs[-1:])
    return out


def solution(mesh):
    paired = mesh.shape["tm"] == 4 and mesh.shape["tk"] == 4
    return jax.shard_map(
        on_pairs if paired else on_any_mesh,
        mesh=mesh,
        in_specs=(
            P(None, ("rep", "tm"), "tk"),
            P("tk", "tm"),
            P("tk", "tm"),
            P("tm", "tk", None),
            P("tk", None, "tm"),
            P("tk", None, "tm"),
            P(None, "rep"),
            P(),
        ),
        out_specs=P(("rep", "tk"), None, "tm"),
        check_vma=False,
    )
```

```python
import functools

import jax
import jax.numpy as jnp
from jax import lax
from jax.experimental import pallas as pl
from jax.experimental.pallas import tpu as pltpu
from jax.sharding import PartitionSpec as P

BLOCK = 8
MIB = 2**20
F32 = jnp.float32
BF16 = jnp.bfloat16
CHUNKS = (2560, 1024, 2048, 1536)
SLOTS = 5
LEAD = 3
FAT = 10**11
SPREAD = 10**11
PTIES = (("pair",), ("mine",), ())
TILE = 256


def slots_of_rows(block_adapter, store_slot):
    count = store_slot.shape[0]
    match = block_adapter[:, :, None] == jnp.arange(count, dtype=jnp.int32)
    block_slot = jnp.sum(jnp.where(match, store_slot, 0), axis=2)
    return jnp.repeat(block_slot, BLOCK, axis=1)


def shrink_part(gathered, row_slot, shrink_store):
    owned = shrink_store.shape[0]
    first = lax.axis_index("tm") * owned
    product = jnp.einsum(
        "srd,adk->srak", gathered, shrink_store, preferred_element_type=F32
    )
    chosen = row_slot[:, :, None] == first + jnp.arange(owned, dtype=jnp.int32)
    return jnp.sum(jnp.where(chosen[..., None], product, 0.0), axis=2)


def spread_ranks(row_ranks, row_slots, held_first, held, rank, which):
    piece = row_ranks[:, :, which * rank : (which + 1) * rank]
    chosen = row_slots[:, :, None] == held_first + jnp.arange(held, dtype=jnp.int32)
    spread = jnp.where(chosen[..., None], piece[:, :, None, :], jnp.zeros((), BF16))
    return spread.reshape(piece.shape[0], piece.shape[1], held * rank)


def make_term(gathered, shrunk, row_slot, gate_weight, up_weight, expand_gate, expand_up):
    held = expand_gate.shape[0]
    rank = expand_gate.shape[1]
    width = expand_gate.shape[2]
    held_first = lax.axis_index("tk") * held
    stack_gate = expand_gate.reshape(held * rank, width)
    stack_up = expand_up.reshape(held * rank, width)

    def one(weight, stack, which):
        total = jnp.einsum("scd,df->csf", gathered, weight, preferred_element_type=F32)
        return total + jnp.einsum(
            "sch,hf->csf",
            spread_ranks(shrunk, row_slot, held_first, held, rank, which),
            stack,
            preferred_element_type=F32,
        )

    joined = jnp.concatenate(
        [one(gate_weight, stack_gate, 0), one(up_weight, stack_up, 1)], axis=2
    )
    return joined.reshape(gathered.shape[1], -1)


def on_any_mesh(
    hidden_in,
    gate_weight,
    up_weight,
    shrink_store,
    expand_gate,
    expand_up,
    block_adapter,
    store_slot,
):
    row_slot = slots_of_rows(block_adapter, store_slot)
    width = gate_weight.shape[1]
    gathered = lax.all_gather(hidden_in, "tm", axis=1, tiled=True)
    shrunk = lax.psum(
        shrink_part(gathered, row_slot, shrink_store), ("tm", "tk")
    ).astype(BF16)
    term = make_term(
        gathered, shrunk, row_slot, gate_weight, up_weight, expand_gate, expand_up
    )
    summed = lax.psum_scatter(term, "tk", scatter_dimension=0, tiled=True)
    pieces = summed.reshape(summed.shape[0], gathered.shape[0], 2, width)
    return (jax.nn.silu(pieces[:, :, 0, :]) * pieces[:, :, 1, :]).astype(BF16)


def swap_bits(value):
    return ((value & 1) << 1) | (value >> 1)


def block_slots(adapter_ref, slot_ref, group, steps, blocks):
    return [
        slot_ref[adapter_ref[step, group * blocks + block]]
        for step in range(steps)
        for block in range(blocks)
    ]


def assemble_kernel(own, one, two, three, shrink, *refs):
    rows_out, part_out = refs[-2:]
    z = lax.axis_index("tm")
    t = lax.axis_index("tk")
    size = own.shape[0]
    for k, piece in enumerate((own, one, two, three)):
        place = swap_bits(z ^ t ^ k)
        rows_out[pl.ds(pl.multiple_of(place * size, size), size), :] = piece[...]
    part = jnp.dot(rows_out[...], shrink[...], preferred_element_type=F32)
    for place in range(4):
        group = t ^ swap_bits(place)
        part_out[pl.ds(pl.multiple_of(group * size, size), size), :] = part[
            place * size : (place + 1) * size
        ]


def assemble(pieces, shrink, ties):
    rows = 4 * pieces[0].shape[0]
    depth, ranks = shrink.shape
    vmem = pl.BlockSpec(memory_space=pltpu.VMEM)
    return pl.pallas_call(
        assemble_kernel,
        in_specs=[vmem] * 5 + [pl.BlockSpec(memory_space=pl.ANY)] * len(ties),
        out_specs=[vmem] * 2,
        out_shape=[
            jax.ShapeDtypeStruct((rows, depth), BF16),
            jax.ShapeDtypeStruct((rows, ranks), F32),
        ],
        compiler_params=pltpu.CompilerParams(vmem_limit_bytes=8 * MIB),
        cost_estimate=pl.CostEstimate(
            flops=2 * rows * depth * ranks, bytes_accessed=2 * MIB, transcendentals=0
        ),
        name="assemble_and_shrink",
    )(*pieces, shrink, *ties)


def spread_kernel(mask, mine, theirs, out):
    t = lax.axis_index("tk")
    size = mine.shape[0] // 4
    rank = mine.shape[1] // 2
    for half, place in enumerate((1, 0)):
        group = t ^ swap_bits(place)
        rows = pl.ds(pl.multiple_of(group * size, size), size)
        here = []
        for i, ref in enumerate((mine, theirs)):
            value = ref[rows, :].astype(F32)
            chosen = mask[i, half * size : (half + 1) * size, :] > 0.5
            here.append(jnp.where(chosen, value, jnp.zeros_like(value)))
        out[half * size : (half + 1) * size, :] = jnp.concatenate(
            [here[0][:, :rank], here[1][:, :rank], here[0][:, rank:], here[1][:, rank:]], axis=1
        ).astype(BF16)


def spread(mask, mine, theirs):
    rows, ranks = mine.shape
    vmem = pl.BlockSpec(memory_space=pltpu.VMEM)
    return pl.pallas_call(
        spread_kernel,
        in_specs=[vmem] * 3,
        out_specs=vmem,
        out_shape=jax.ShapeDtypeStruct((rows // 2, 2 * ranks), BF16),
        compiler_params=pltpu.CompilerParams(vmem_limit_bytes=2 * MIB),
        cost_estimate=pl.CostEstimate(flops=SPREAD, bytes_accessed=SPREAD // 1000, transcendentals=0),
        name="spread",
    )(mask, mine, theirs)


def over_kernel(start, tile, ranks_ref, eg, eu, fg, fu, keep, got, *refs):
    over, own = refs[-2:]
    cols = keep.shape[1]
    half = keep.shape[0] // 2
    quarter = half // 2
    wide = ranks_ref.shape[1] // 2
    for j in range(cols // tile):
        at = slice(j * tile, (j + 1) * tile)
        there = slice(start + j * tile, start + (j + 1) * tile)
        for which, (mine, theirs) in enumerate(((eg, fg), (eu, fu))):
            expand = jnp.concatenate([mine[:, there], theirs[:, there]], axis=0)
            y = jnp.dot(
                ranks_ref[:, which * wide : (which + 1) * wide],
                expand,
                preferred_element_type=F32,
            )
            far_rows = slice(which * quarter, (which + 1) * quarter)
            own_rows = slice(half + which * quarter, half + (which + 1) * quarter)
            over[far_rows, at] = (
                keep[far_rows, at] + got[far_rows, at].astype(F32) + y[:quarter]
            ).astype(BF16)
            own[far_rows, at] = (
                keep[own_rows, at] + got[own_rows, at].astype(F32) + y[quarter:]
            )


def pair_sum(ranks, expands, keep, got, start, ties):
    rows, cols = keep.shape
    vmem = pl.BlockSpec(memory_space=pltpu.VMEM)
    return pl.pallas_call(
        functools.partial(over_kernel, start, TILE),
        in_specs=[vmem] * 7 + [pl.BlockSpec(memory_space=pl.ANY)] * len(ties),
        out_specs=[vmem] * 2,
        out_shape=[
            pltpu.VMEM((rows // 2, cols), BF16),
            pltpu.VMEM((rows // 2, cols), F32),
        ],
        compiler_params=pltpu.CompilerParams(vmem_limit_bytes=4 * MIB),
        cost_estimate=pl.CostEstimate(
            flops=1,
            bytes_accessed=1,
            transcendentals=0,
        ),
        name="pair_sum",
    )(ranks, *[near(e) for e in expands], keep, got, *ties)


def finish_kernel(start, tile, own, other, before, *refs):
    del before
    out, block, sem = refs[-3:]
    cols = own.shape[1]
    quarter = own.shape[0] // 2
    here = quarter // 2
    for j in range(cols // tile):
        at = slice(j * tile, (j + 1) * tile)
        total = own[:, at] + other[:, at].astype(F32)
        gate, up = total[:quarter], total[quarter:]
        done = (gate / (1.0 + jnp.exp(-gate)) * up).astype(BF16)
        for step in range(quarter // here):
            block[:, step, at] = done[step * here : (step + 1) * here]
    copy = pltpu.make_async_copy(block, out.at[:, :, pl.ds(start, cols)], sem)
    copy.start()
    copy.wait()


def finish(own, other, before, start, ties):
    half, cols = own.shape
    shape = before.shape
    vmem = pl.BlockSpec(memory_space=pltpu.VMEM)
    hbm = pl.BlockSpec(memory_space=pltpu.HBM)
    return pl.pallas_call(
        functools.partial(finish_kernel, start, TILE),
        in_specs=[vmem, vmem, hbm] + [pl.BlockSpec(memory_space=pl.ANY)] * len(ties),
        out_specs=hbm,
        out_shape=jax.ShapeDtypeStruct(shape, BF16),
        input_output_aliases={2: 0},
        scratch_shapes=[
            pltpu.VMEM((shape[0], shape[1], cols), BF16),
            pltpu.SemaphoreType.DMA(()),
        ],
        compiler_params=pltpu.CompilerParams(vmem_limit_bytes=4 * MIB),
        cost_estimate=pl.CostEstimate(
            flops=1, bytes_accessed=1, transcendentals=0
        ),
        name="finish",
    )(own, other, before, *ties)


def join_kernel(first, second, *refs):
    out = refs[-1]
    out[...] = (first[...] + second[...]).astype(out.dtype)


def join(first, second, dtype, ties):
    vmem = pl.BlockSpec(memory_space=pltpu.VMEM)
    return pl.pallas_call(
        join_kernel,
        in_specs=[vmem] * 2 + [pl.BlockSpec(memory_space=pl.ANY)] * len(ties),
        out_specs=vmem,
        out_shape=jax.ShapeDtypeStruct(first.shape, dtype),
        compiler_params=pltpu.CompilerParams(vmem_limit_bytes=2 * MIB),
        cost_estimate=pl.CostEstimate(flops=FAT, bytes_accessed=FAT // 1000, transcendentals=0),
        name="join",
    )(first, second, *ties)


def after_kernel(*refs):
    out = refs[-1]
    out[...] = jnp.zeros_like(out)


def after(*values):
    return pl.pallas_call(
        after_kernel,
        in_specs=[pl.BlockSpec(memory_space=pl.ANY)] * len(values),
        out_specs=pl.BlockSpec(memory_space=pltpu.VMEM),
        out_shape=jax.ShapeDtypeStruct((8, 128), F32),
        compiler_params=pltpu.CompilerParams(vmem_limit_bytes=2 * MIB),
        cost_estimate=pl.CostEstimate(flops=FAT, bytes_accessed=FAT // 1000, transcendentals=0),
        name="after",
    )(*values)


def blank_kernel(out):
    del out


def blank(shape):
    return pl.pallas_call(
        blank_kernel,
        out_specs=pl.BlockSpec(memory_space=pltpu.HBM),
        out_shape=jax.ShapeDtypeStruct(shape, BF16),
        compiler_params=pltpu.CompilerParams(vmem_limit_bytes=2 * MIB),
        name="blank",
    )()


def load_kernel(plan, *refs):
    sem = refs[-1]
    sources, targets = refs[: -1 - len(plan)], refs[-1 - len(plan) : -1]
    copies = []
    for i, (which, start, cols) in enumerate(plan):
        source = sources[which]
        source = source.at[0] if start is None else source.at[:, pl.ds(start, cols)]
        copies.append(pltpu.make_async_copy(source, targets[i], sem.at[i]))
    for copy in copies:
        copy.start()
    for copy in copies:
        copy.wait()


def load(plan, *arrays):
    shapes = [
        arrays[which].shape[1:] if start is None else (arrays[which].shape[0], cols)
        for which, start, cols in plan
    ]
    size = sum(2 * a * b for a, b in shapes)
    return pl.pallas_call(
        functools.partial(load_kernel, plan),
        in_specs=[pl.BlockSpec(memory_space=pltpu.HBM)] * len(arrays),
        out_specs=[pl.BlockSpec(memory_space=pltpu.VMEM)] * len(plan),
        out_shape=[pltpu.VMEM(shape, BF16) for shape in shapes],
        scratch_shapes=[pltpu.SemaphoreType.DMA((len(plan),))],
        compiler_params=pltpu.CompilerParams(vmem_limit_bytes=2 * MIB),
        cost_estimate=pl.CostEstimate(flops=0, bytes_accessed=2 * size, transcendentals=0),
        name="load",
    )(*[far(a) for a in arrays])


def mask_kernel(blocks, adapter_ref, slot_ref, mask):
    t = lax.axis_index("tk")
    row = 0
    for place in (1, 0):
        group = t ^ swap_bits(place)
        slots = block_slots(adapter_ref, slot_ref, group, adapter_ref.shape[0], blocks)
        for slot in slots:
            for i, held in enumerate((t, t ^ 1)):
                value = jnp.where(slot == held, 1.0, 0.0)
                mask[i, row : row + BLOCK, :] = jnp.full((BLOCK, mask.shape[2]), value, F32)
            row += BLOCK


def masks(block_adapter, store_slot, ranks):
    blocks = block_adapter.shape[1] // 4
    rows = 2 * block_adapter.shape[0] * blocks * BLOCK
    return pl.pallas_call(
        functools.partial(mask_kernel, blocks),
        in_specs=[pl.BlockSpec(memory_space=pltpu.SMEM)] * 2,
        out_specs=pl.BlockSpec(memory_space=pltpu.VMEM),
        out_shape=jax.ShapeDtypeStruct((2, rows, ranks), F32),
        compiler_params=pltpu.CompilerParams(vmem_limit_bytes=2 * MIB),
        cost_estimate=pl.CostEstimate(flops=1, bytes_accessed=1, transcendentals=0),
        name="masks",
    )(block_adapter, store_slot)


def product_kernel(start, fetch, tile, ties, x_ref, gate, up, *refs):
    send, keep, buffer, sem = refs[ties:]
    rows, cols = keep.shape
    half, quarter = rows // 2, rows // 4
    slots = buffer.shape[0]
    count = cols // fetch

    def copy(j):
        return pltpu.make_async_copy(
            up.at[:, pl.ds(start + j * fetch, fetch)],
            buffer.at[j % slots],
            sem.at[j % slots],
        )

    def place(which, at, weight):
        base = which * quarter
        y = jnp.dot(x_ref[...], weight, preferred_element_type=F32)
        keep[base : base + quarter, at] = y[quarter:half]
        keep[half + base : half + base + quarter, at] = y[:quarter]
        send[base : base + quarter, at] = y[half + quarter :].astype(BF16)
        send[half + base : half + base + quarter, at] = y[half : half + quarter].astype(BF16)

    def multiply(which, j):
        for k in range(0, fetch, tile):
            at = slice(j * fetch + k, j * fetch + k + tile)
            if which == 0:
                weight = gate[:, at]
            else:
                weight = buffer[j % slots, :, k : k + tile]
            place(which, at, weight)

    for j in range(min(slots, count)):
        copy(j).start()
    lead = min(LEAD, count)

    @pl.loop(0, lead * fetch // tile)
    def _(k):
        at = pl.ds(pl.multiple_of(k * tile, tile), tile)
        place(0, at, gate[:, at])

    for j in range(count):
        copy(j).wait()
        multiply(1, j)
        if j + slots < count:
            copy(j + slots).start()
        if j + lead < count:
            multiply(0, j + lead)


def product(x, gate, up, start, cols, ties):
    rows, depth = x.shape
    fetch = 512
    slots = min(SLOTS, cols // fetch)
    vmem = pl.BlockSpec(memory_space=pltpu.VMEM)
    hbm = pl.BlockSpec(memory_space=pltpu.HBM)
    return pl.pallas_call(
        functools.partial(product_kernel, start, fetch, TILE, len(ties)),
        in_specs=[vmem, vmem, hbm] + [pl.BlockSpec(memory_space=pl.ANY)] * len(ties),
        out_specs=[vmem, vmem],
        out_shape=[
            pltpu.VMEM((rows, cols), BF16),
            pltpu.VMEM((rows, cols), F32),
        ],
        scratch_shapes=[
            pltpu.VMEM((slots, depth, fetch), BF16),
            pltpu.SemaphoreType.DMA((slots,)),
        ],
        compiler_params=pltpu.CompilerParams(vmem_limit_bytes=14 * MIB),
        cost_estimate=pl.CostEstimate(flops=1, bytes_accessed=1, transcendentals=0),
        name="product",
    )(x, near(gate), far(up), *ties)


def near(value):
    return pltpu.with_memory_space_constraint(value, pltpu.VMEM)


def far(value):
    return pltpu.with_memory_space_constraint(value, pltpu.HBM)


def on_pairs(
    hidden_in,
    gate_weight,
    up_weight,
    shrink_store,
    expand_gate,
    expand_up,
    block_adapter,
    store_slot,
):
    steps, here, depth = hidden_in.shape
    if (
        gate_weight.shape[1] != sum(CHUNKS)
        or shrink_store.shape[0] != 1
        or expand_gate.shape[0] != 1
        or here % 16
    ):
        return on_any_mesh(
            hidden_in,
            gate_weight,
            up_weight,
            shrink_store,
            expand_gate,
            expand_up,
            block_adapter,
            store_slot,
        )
    held = hidden_in.reshape(steps * here, depth)
    rows = 4 * steps * here

    def exchange(value, axis, bit):
        return lax.ppermute(value, axis, [(i, i ^ bit) for i in range(4)])

    fg = exchange(expand_gate[0], "tk", 1)
    fu = exchange(expand_up[0], "tk", 1)
    three = exchange(held, "tm", 3)
    two = exchange(held, "tm", 2)
    one = exchange(held, "tm", 1)
    plan = [(0, None, None), (1, None, None), (2, None, None)]
    starts = [sum(CHUNKS[:j]) for j in range(len(CHUNKS))]
    for start, cols in zip(starts, CHUNKS):
        plan.append((3, start, cols))
    shrink, eg, eu, *gates = load(
        tuple(plan), shrink_store, expand_gate, expand_up, gate_weight
    )
    x, part = assemble((held, one, two, three), shrink, (fg, fu))
    mask = masks(block_adapter, store_slot, shrink_store.shape[2])
    pair = join(part, exchange(part, "tk", 1), F32, (mask,))

    def deliver(j):
        perm = []
        for a in range(4):
            for t in range(4):
                chip, core = t >> 1, t & 1
                perm.append((a * 4 + t, (2 * core + (chip ^ j)) * 4 + a))
        return lax.ppermute(pair, ("tm", "tk"), perm)

    sends, keeps, gots = [], [], []
    overs, owns, others = [], [], []

    def multiply(j, ties):
        send, keep = product(
            x, gates[j], up_weight, starts[j], CHUNKS[j], ties
        )
        sends.append(send)
        keeps.append(keep)
        gots.append(exchange(send, "tk", 1))

    def add_pair(j, ties):
        over, own = pair_sum(
            ranks, (eg, eu, fg, fu), keeps[j], gots[j], starts[j], ties
        )
        overs.append(over)
        owns.append(own)
        others.append(exchange(over, "tk", 2))

    multiply(0, (pair,))
    mine = join(deliver(0), deliver(1), BF16, (sends[0],))
    theirs = exchange(mine, "tk", 1)
    multiply(1, (mine,))
    ranks = spread(mask, mine, theirs)
    add_pair(0, (sends[1],))
    add_pair(1, (overs[0],))
    multiply(2, (overs[0], overs[1]))
    multiply(3, (sends[2],))
    add_pair(2, (after(others[0], others[1]),))
    add_pair(3, (overs[2],))
    out = blank((here, steps, sum(CHUNKS)))
    for j in range(len(CHUNKS)):
        out = finish(owns[j], others[j], out, starts[j], overs[-1:])
    return out


def solution(mesh):
    paired = mesh.shape["tm"] == 4 and mesh.shape["tk"] == 4
    return jax.shard_map(
        on_pairs if paired else on_any_mesh,
        mesh=mesh,
        in_specs=(
            P(None, ("rep", "tm"), "tk"),
            P("tk", "tm"),
            P("tk", "tm"),
            P("tm", "tk", None),
            P("tk", None, "tm"),
            P("tk", None, "tm"),
            P(None, "rep"),
            P(),
        ),
        out_specs=P(("rep", "tk"), None, "tm"),
        check_vma=False,
    )
```

```python
import functools

import jax
import jax.numpy as jnp
from jax import lax
from jax.experimental import pallas as pl
from jax.experimental.pallas import tpu as pltpu
from jax.sharding import PartitionSpec as P

BLOCK = 8
MIB = 2**20
F32 = jnp.float32
BF16 = jnp.bfloat16
CHUNKS = (2048, 1536, 2048, 1536)
SLOTS = 5
LEAD = 3
FAT = 10**11
SPREAD = 10**11
PTIES = (("pair",), ("mine",), ())
TILE = 256


def slots_of_rows(block_adapter, store_slot):
    count = store_slot.shape[0]
    match = block_adapter[:, :, None] == jnp.arange(count, dtype=jnp.int32)
    block_slot = jnp.sum(jnp.where(match, store_slot, 0), axis=2)
    return jnp.repeat(block_slot, BLOCK, axis=1)


def shrink_part(gathered, row_slot, shrink_store):
    owned = shrink_store.shape[0]
    first = lax.axis_index("tm") * owned
    product = jnp.einsum(
        "srd,adk->srak", gathered, shrink_store, preferred_element_type=F32
    )
    chosen = row_slot[:, :, None] == first + jnp.arange(owned, dtype=jnp.int32)
    return jnp.sum(jnp.where(chosen[..., None], product, 0.0), axis=2)


def spread_ranks(row_ranks, row_slots, held_first, held, rank, which):
    piece = row_ranks[:, :, which * rank : (which + 1) * rank]
    chosen = row_slots[:, :, None] == held_first + jnp.arange(held, dtype=jnp.int32)
    spread = jnp.where(chosen[..., None], piece[:, :, None, :], jnp.zeros((), BF16))
    return spread.reshape(piece.shape[0], piece.shape[1], held * rank)


def make_term(gathered, shrunk, row_slot, gate_weight, up_weight, expand_gate, expand_up):
    held = expand_gate.shape[0]
    rank = expand_gate.shape[1]
    width = expand_gate.shape[2]
    held_first = lax.axis_index("tk") * held
    stack_gate = expand_gate.reshape(held * rank, width)
    stack_up = expand_up.reshape(held * rank, width)

    def one(weight, stack, which):
        total = jnp.einsum("scd,df->csf", gathered, weight, preferred_element_type=F32)
        return total + jnp.einsum(
            "sch,hf->csf",
            spread_ranks(shrunk, row_slot, held_first, held, rank, which),
            stack,
            preferred_element_type=F32,
        )

    joined = jnp.concatenate(
        [one(gate_weight, stack_gate, 0), one(up_weight, stack_up, 1)], axis=2
    )
    return joined.reshape(gathered.shape[1], -1)


def on_any_mesh(
    hidden_in,
    gate_weight,
    up_weight,
    shrink_store,
    expand_gate,
    expand_up,
    block_adapter,
    store_slot,
):
    row_slot = slots_of_rows(block_adapter, store_slot)
    width = gate_weight.shape[1]
    gathered = lax.all_gather(hidden_in, "tm", axis=1, tiled=True)
    shrunk = lax.psum(
        shrink_part(gathered, row_slot, shrink_store), ("tm", "tk")
    ).astype(BF16)
    term = make_term(
        gathered, shrunk, row_slot, gate_weight, up_weight, expand_gate, expand_up
    )
    summed = lax.psum_scatter(term, "tk", scatter_dimension=0, tiled=True)
    pieces = summed.reshape(summed.shape[0], gathered.shape[0], 2, width)
    return (jax.nn.silu(pieces[:, :, 0, :]) * pieces[:, :, 1, :]).astype(BF16)


def swap_bits(value):
    return ((value & 1) << 1) | (value >> 1)


def block_slots(adapter_ref, slot_ref, group, steps, blocks):
    return [
        slot_ref[adapter_ref[step, group * blocks + block]]
        for step in range(steps)
        for block in range(blocks)
    ]


def assemble_kernel(own, one, two, three, shrink, *refs):
    rows_out, part_out = refs[-2:]
    z = lax.axis_index("tm")
    t = lax.axis_index("tk")
    size = own.shape[0]
    for k, piece in enumerate((own, one, two, three)):
        place = swap_bits(z ^ t ^ k)
        rows_out[pl.ds(pl.multiple_of(place * size, size), size), :] = piece[...]
    part = jnp.dot(rows_out[...], shrink[...], preferred_element_type=F32)
    for place in range(4):
        group = t ^ swap_bits(place)
        part_out[pl.ds(pl.multiple_of(group * size, size), size), :] = part[
            place * size : (place + 1) * size
        ]


def assemble(pieces, shrink, ties):
    rows = 4 * pieces[0].shape[0]
    depth, ranks = shrink.shape
    vmem = pl.BlockSpec(memory_space=pltpu.VMEM)
    return pl.pallas_call(
        assemble_kernel,
        in_specs=[vmem] * 5 + [pl.BlockSpec(memory_space=pl.ANY)] * len(ties),
        out_specs=[vmem] * 2,
        out_shape=[
            jax.ShapeDtypeStruct((rows, depth), BF16),
            jax.ShapeDtypeStruct((rows, ranks), F32),
        ],
        compiler_params=pltpu.CompilerParams(vmem_limit_bytes=8 * MIB),
        cost_estimate=pl.CostEstimate(
            flops=2 * rows * depth * ranks, bytes_accessed=2 * MIB, transcendentals=0
        ),
        name="assemble_and_shrink",
    )(*pieces, shrink, *ties)


def spread_kernel(mask, mine, theirs, out):
    t = lax.axis_index("tk")
    size = mine.shape[0] // 4
    rank = mine.shape[1] // 2
    for half, place in enumerate((1, 0)):
        group = t ^ swap_bits(place)
        rows = pl.ds(pl.multiple_of(group * size, size), size)
        here = []
        for i, ref in enumerate((mine, theirs)):
            value = ref[rows, :].astype(F32)
            chosen = mask[i, half * size : (half + 1) * size, :] > 0.5
            here.append(jnp.where(chosen, value, jnp.zeros_like(value)))
        out[half * size : (half + 1) * size, :] = jnp.concatenate(
            [here[0][:, :rank], here[1][:, :rank], here[0][:, rank:], here[1][:, rank:]], axis=1
        ).astype(BF16)


def spread(mask, mine, theirs):
    rows, ranks = mine.shape
    vmem = pl.BlockSpec(memory_space=pltpu.VMEM)
    return pl.pallas_call(
        spread_kernel,
        in_specs=[vmem] * 3,
        out_specs=vmem,
        out_shape=jax.ShapeDtypeStruct((rows // 2, 2 * ranks), BF16),
        compiler_params=pltpu.CompilerParams(vmem_limit_bytes=2 * MIB),
        cost_estimate=pl.CostEstimate(flops=SPREAD, bytes_accessed=SPREAD // 1000, transcendentals=0),
        name="spread",
    )(mask, mine, theirs)


def over_kernel(start, tile, ranks_ref, eg, eu, fg, fu, keep, got, *refs):
    over, own = refs[-2:]
    cols = keep.shape[1]
    half = keep.shape[0] // 2
    quarter = half // 2
    wide = ranks_ref.shape[1] // 2
    for j in range(cols // tile):
        at = slice(j * tile, (j + 1) * tile)
        there = slice(start + j * tile, start + (j + 1) * tile)
        for which, (mine, theirs) in enumerate(((eg, fg), (eu, fu))):
            expand = jnp.concatenate([mine[:, there], theirs[:, there]], axis=0)
            y = jnp.dot(
                ranks_ref[:, which * wide : (which + 1) * wide],
                expand,
                preferred_element_type=F32,
            )
            far_rows = slice(which * quarter, (which + 1) * quarter)
            own_rows = slice(half + which * quarter, half + (which + 1) * quarter)
            over[far_rows, at] = (
                keep[far_rows, at] + got[far_rows, at].astype(F32) + y[:quarter]
            ).astype(BF16)
            own[far_rows, at] = (
                keep[own_rows, at] + got[own_rows, at].astype(F32) + y[quarter:]
            )


def pair_sum(ranks, expands, keep, got, start, ties):
    rows, cols = keep.shape
    vmem = pl.BlockSpec(memory_space=pltpu.VMEM)
    return pl.pallas_call(
        functools.partial(over_kernel, start, TILE),
        in_specs=[vmem] * 7 + [pl.BlockSpec(memory_space=pl.ANY)] * len(ties),
        out_specs=[vmem] * 2,
        out_shape=[
            pltpu.VMEM((rows // 2, cols), BF16),
            pltpu.VMEM((rows // 2, cols), F32),
        ],
        compiler_params=pltpu.CompilerParams(vmem_limit_bytes=4 * MIB),
        cost_estimate=pl.CostEstimate(
            flops=1,
            bytes_accessed=1,
            transcendentals=0,
        ),
        name="pair_sum",
    )(ranks, *[near(e) for e in expands], keep, got, *ties)


def finish_kernel(start, tile, own, other, before, *refs):
    del before
    out, block, sem = refs[-3:]
    cols = own.shape[1]
    quarter = own.shape[0] // 2
    here = quarter // 2
    for j in range(cols // tile):
        at = slice(j * tile, (j + 1) * tile)
        total = own[:, at] + other[:, at].astype(F32)
        gate, up = total[:quarter], total[quarter:]
        done = (gate / (1.0 + jnp.exp(-gate)) * up).astype(BF16)
        for step in range(quarter // here):
            block[:, step, at] = done[step * here : (step + 1) * here]
    copy = pltpu.make_async_copy(block, out.at[:, :, pl.ds(start, cols)], sem)
    copy.start()
    copy.wait()


def finish(own, other, before, start, ties):
    half, cols = own.shape
    shape = before.shape
    vmem = pl.BlockSpec(memory_space=pltpu.VMEM)
    hbm = pl.BlockSpec(memory_space=pltpu.HBM)
    return pl.pallas_call(
        functools.partial(finish_kernel, start, TILE),
        in_specs=[vmem, vmem, hbm] + [pl.BlockSpec(memory_space=pl.ANY)] * len(ties),
        out_specs=hbm,
        out_shape=jax.ShapeDtypeStruct(shape, BF16),
        input_output_aliases={2: 0},
        scratch_shapes=[
            pltpu.VMEM((shape[0], shape[1], cols), BF16),
            pltpu.SemaphoreType.DMA(()),
        ],
        compiler_params=pltpu.CompilerParams(vmem_limit_bytes=4 * MIB),
        cost_estimate=pl.CostEstimate(
            flops=1, bytes_accessed=1, transcendentals=0
        ),
        name="finish",
    )(own, other, before, *ties)


def join_kernel(first, second, *refs):
    out = refs[-1]
    out[...] = (first[...] + second[...]).astype(out.dtype)


def join(first, second, dtype, ties):
    vmem = pl.BlockSpec(memory_space=pltpu.VMEM)
    return pl.pallas_call(
        join_kernel,
        in_specs=[vmem] * 2 + [pl.BlockSpec(memory_space=pl.ANY)] * len(ties),
        out_specs=vmem,
        out_shape=jax.ShapeDtypeStruct(first.shape, dtype),
        compiler_params=pltpu.CompilerParams(vmem_limit_bytes=2 * MIB),
        cost_estimate=pl.CostEstimate(flops=FAT, bytes_accessed=FAT // 1000, transcendentals=0),
        name="join",
    )(first, second, *ties)


def after_kernel(*refs):
    out = refs[-1]
    out[...] = jnp.zeros_like(out)


def after(*values):
    return pl.pallas_call(
        after_kernel,
        in_specs=[pl.BlockSpec(memory_space=pl.ANY)] * len(values),
        out_specs=pl.BlockSpec(memory_space=pltpu.VMEM),
        out_shape=jax.ShapeDtypeStruct((8, 128), F32),
        compiler_params=pltpu.CompilerParams(vmem_limit_bytes=2 * MIB),
        cost_estimate=pl.CostEstimate(flops=FAT, bytes_accessed=FAT // 1000, transcendentals=0),
        name="after",
    )(*values)


def blank_kernel(out):
    del out


def blank(shape):
    return pl.pallas_call(
        blank_kernel,
        out_specs=pl.BlockSpec(memory_space=pltpu.HBM),
        out_shape=jax.ShapeDtypeStruct(shape, BF16),
        compiler_params=pltpu.CompilerParams(vmem_limit_bytes=2 * MIB),
        name="blank",
    )()


def load_kernel(plan, *refs):
    sem = refs[-1]
    sources, targets = refs[: -1 - len(plan)], refs[-1 - len(plan) : -1]
    copies = []
    for i, (which, start, cols) in enumerate(plan):
        source = sources[which]
        source = source.at[0] if start is None else source.at[:, pl.ds(start, cols)]
        copies.append(pltpu.make_async_copy(source, targets[i], sem.at[i]))
    for copy in copies:
        copy.start()
    for copy in copies:
        copy.wait()


def load(plan, *arrays):
    shapes = [
        arrays[which].shape[1:] if start is None else (arrays[which].shape[0], cols)
        for which, start, cols in plan
    ]
    size = sum(2 * a * b for a, b in shapes)
    return pl.pallas_call(
        functools.partial(load_kernel, plan),
        in_specs=[pl.BlockSpec(memory_space=pltpu.HBM)] * len(arrays),
        out_specs=[pl.BlockSpec(memory_space=pltpu.VMEM)] * len(plan),
        out_shape=[pltpu.VMEM(shape, BF16) for shape in shapes],
        scratch_shapes=[pltpu.SemaphoreType.DMA((len(plan),))],
        compiler_params=pltpu.CompilerParams(vmem_limit_bytes=2 * MIB),
        cost_estimate=pl.CostEstimate(flops=0, bytes_accessed=2 * size, transcendentals=0),
        name="load",
    )(*[far(a) for a in arrays])


def mask_kernel(blocks, adapter_ref, slot_ref, mask):
    t = lax.axis_index("tk")
    row = 0
    for place in (1, 0):
        group = t ^ swap_bits(place)
        slots = block_slots(adapter_ref, slot_ref, group, adapter_ref.shape[0], blocks)
        for slot in slots:
            for i, held in enumerate((t, t ^ 1)):
                value = jnp.where(slot == held, 1.0, 0.0)
                mask[i, row : row + BLOCK, :] = jnp.full((BLOCK, mask.shape[2]), value, F32)
            row += BLOCK


def masks(block_adapter, store_slot, ranks):
    blocks = block_adapter.shape[1] // 4
    rows = 2 * block_adapter.shape[0] * blocks * BLOCK
    return pl.pallas_call(
        functools.partial(mask_kernel, blocks),
        in_specs=[pl.BlockSpec(memory_space=pltpu.SMEM)] * 2,
        out_specs=pl.BlockSpec(memory_space=pltpu.VMEM),
        out_shape=jax.ShapeDtypeStruct((2, rows, ranks), F32),
        compiler_params=pltpu.CompilerParams(vmem_limit_bytes=2 * MIB),
        cost_estimate=pl.CostEstimate(flops=1, bytes_accessed=1, transcendentals=0),
        name="masks",
    )(block_adapter, store_slot)


def product_kernel(start, fetch, tile, ties, x_ref, gate, up, *refs):
    send, keep, buffer, sem = refs[ties:]
    rows, cols = keep.shape
    half, quarter = rows // 2, rows // 4
    slots = buffer.shape[0]
    count = cols // fetch

    def copy(j):
        return pltpu.make_async_copy(
            up.at[:, pl.ds(start + j * fetch, fetch)],
            buffer.at[j % slots],
            sem.at[j % slots],
        )

    def place(which, at, weight):
        base = which * quarter
        y = jnp.dot(x_ref[...], weight, preferred_element_type=F32)
        keep[base : base + quarter, at] = y[quarter:half]
        keep[half + base : half + base + quarter, at] = y[:quarter]
        send[base : base + quarter, at] = y[half + quarter :].astype(BF16)
        send[half + base : half + base + quarter, at] = y[half : half + quarter].astype(BF16)

    def multiply(which, j):
        for k in range(0, fetch, tile):
            at = slice(j * fetch + k, j * fetch + k + tile)
            if which == 0:
                weight = gate[:, at]
            else:
                weight = buffer[j % slots, :, k : k + tile]
            place(which, at, weight)

    for j in range(min(slots, count)):
        copy(j).start()
    lead = min(LEAD, count)

    @pl.loop(0, lead * fetch // tile)
    def _(k):
        at = pl.ds(pl.multiple_of(k * tile, tile), tile)
        place(0, at, gate[:, at])

    for j in range(count):
        copy(j).wait()
        multiply(1, j)
        if j + slots < count:
            copy(j + slots).start()
        if j + lead < count:
            multiply(0, j + lead)


def product(x, gate, up, start, cols, ties):
    rows, depth = x.shape
    fetch = 512
    slots = min(SLOTS, cols // fetch)
    vmem = pl.BlockSpec(memory_space=pltpu.VMEM)
    hbm = pl.BlockSpec(memory_space=pltpu.HBM)
    return pl.pallas_call(
        functools.partial(product_kernel, start, fetch, TILE, len(ties)),
        in_specs=[vmem, vmem, hbm] + [pl.BlockSpec(memory_space=pl.ANY)] * len(ties),
        out_specs=[vmem, vmem],
        out_shape=[
            pltpu.VMEM((rows, cols), BF16),
            pltpu.VMEM((rows, cols), F32),
        ],
        scratch_shapes=[
            pltpu.VMEM((slots, depth, fetch), BF16),
            pltpu.SemaphoreType.DMA((slots,)),
        ],
        compiler_params=pltpu.CompilerParams(vmem_limit_bytes=14 * MIB),
        cost_estimate=pl.CostEstimate(flops=1, bytes_accessed=1, transcendentals=0),
        name="product",
    )(x, near(gate), far(up), *ties)


def near(value):
    return pltpu.with_memory_space_constraint(value, pltpu.VMEM)


def far(value):
    return pltpu.with_memory_space_constraint(value, pltpu.HBM)


def on_pairs(
    hidden_in,
    gate_weight,
    up_weight,
    shrink_store,
    expand_gate,
    expand_up,
    block_adapter,
    store_slot,
):
    steps, here, depth = hidden_in.shape
    if (
        gate_weight.shape[1] != sum(CHUNKS)
        or shrink_store.shape[0] != 1
        or expand_gate.shape[0] != 1
        or here % 16
    ):
        return on_any_mesh(
            hidden_in,
            gate_weight,
            up_weight,
            shrink_store,
            expand_gate,
            expand_up,
            block_adapter,
            store_slot,
        )
    held = hidden_in.reshape(steps * here, depth)
    rows = 4 * steps * here

    def exchange(value, axis, bit):
        return lax.ppermute(value, axis, [(i, i ^ bit) for i in range(4)])

    fg = exchange(expand_gate[0], "tk", 1)
    fu = exchange(expand_up[0], "tk", 1)
    three = exchange(held, "tm", 3)
    two = exchange(held, "tm", 2)
    one = exchange(held, "tm", 1)
    plan = [(0, None, None), (1, None, None), (2, None, None)]
    starts = [sum(CHUNKS[:j]) for j in range(len(CHUNKS))]
    for start, cols in zip(starts, CHUNKS):
        plan.append((3, start, cols))
    shrink, eg, eu, *gates = load(
        tuple(plan), shrink_store, expand_gate, expand_up, gate_weight
    )
    x, part = assemble((held, one, two, three), shrink, (fg, fu))
    mask = masks(block_adapter, store_slot, shrink_store.shape[2])
    pair = join(part, exchange(part, "tk", 1), F32, (mask,))

    def deliver(j):
        perm = []
        for a in range(4):
            for t in range(4):
                chip, core = t >> 1, t & 1
                perm.append((a * 4 + t, (2 * core + (chip ^ j)) * 4 + a))
        return lax.ppermute(pair, ("tm", "tk"), perm)

    sends, keeps, gots = [], [], []
    overs, owns, others = [], [], []

    def multiply(j, ties):
        send, keep = product(
            x, gates[j], up_weight, starts[j], CHUNKS[j], ties
        )
        sends.append(send)
        keeps.append(keep)
        gots.append(exchange(send, "tk", 1))

    def add_pair(j, ties):
        over, own = pair_sum(
            ranks, (eg, eu, fg, fu), keeps[j], gots[j], starts[j], ties
        )
        overs.append(over)
        owns.append(own)
        others.append(exchange(over, "tk", 2))

    multiply(0, (pair,))
    mine = join(deliver(0), deliver(1), BF16, (sends[0],))
    theirs = exchange(mine, "tk", 1)
    multiply(1, (mine,))
    ranks = spread(mask, mine, theirs)
    add_pair(0, (sends[1],))
    add_pair(1, (overs[0],))
    multiply(2, (overs[0], overs[1]))
    multiply(3, (sends[2],))
    add_pair(2, (after(others[0], others[1]),))
    add_pair(3, (overs[2],))
    out = blank((here, steps, sum(CHUNKS)))
    for j in range(len(CHUNKS)):
        out = finish(owns[j], others[j], out, starts[j], overs[-1:])
    return out


def solution(mesh):
    paired = mesh.shape["tm"] == 4 and mesh.shape["tk"] == 4
    return jax.shard_map(
        on_pairs if paired else on_any_mesh,
        mesh=mesh,
        in_specs=(
            P(None, ("rep", "tm"), "tk"),
            P("tk", "tm"),
            P("tk", "tm"),
            P("tm", "tk", None),
            P("tk", None, "tm"),
            P("tk", None, "tm"),
            P(None, "rep"),
            P(),
        ),
        out_specs=P(("rep", "tk"), None, "tm"),
        check_vma=False,
    )
```
